32 devices in a mesh: section: 2 (over y), expert: 16 (over z, x, core).
Axes of the slice: x: 2, y: 2, z: 4, core: 2. Of those that a mesh axis runs over, the one named last changes fastest.
Arguments:
- tokens: bfloat16 [2048, 3584], P('expert'), may hold values from -6 to 6
- norm_gain: bfloat16 [3584], replicated, may hold values from 0.25 to 1.75
- router: bfloat16 [3584, 16], replicated, may hold values from -0.09375 to 0.09375
- w_gate: bfloat16 [16, 3584, 1024], P('expert', None, 'section'), may hold values from -0.09375 to 0.09375
- w_up: bfloat16 [16, 3584, 1024], P('expert', None, 'section'), may hold values from -0.09375 to 0.09375
- w_down: bfloat16 [16, 1024, 3584], P('expert', 'section'), may hold values from -0.1875 to 0.1875
- expert_ids: int32 [2048, 3], P('expert'), may hold values from 0 to 15, all different within a row; in each aligned block of 128 rows (0 to 127, 128 to 255, ...) at most 36 rows name the same one
Outputs:
- layer_out: bfloat16 [2048, 3584], P('expert', 'section')
The draws below stay inside these ranges and needn't reach their ends.
Inputs may be any that keep to these rules, and one draw needn't show every extreme that they name: `expert_ids`: each row names 3 different experts. Within each aligned block of 128 rows (the rows of one index of the expert axis) no expert is named by more than 36 rows, and in every draw some expert is named by exactly 36 rows of some block.
All inputs are finite; a program needn't handle non-finite values.
Results may differ from the reference program's by a relative error of at most 0.013.
Values may be sent and summed in bfloat16 or wider, within the bound.
No kernel may reach another device: no remote copies, remote signals or barrier semaphores. Data moves between devices by JAX's collectives and lax.ppermute only.
A program may use at most 64 MiB of HBM per device.

```python
import math
import jax
import jax.numpy as jnp
import numpy as np
from jax import lax

D = 3584
FF = 1024
TOP = 3
TOK_DEV = 128
EXPERTS = 16
TOKENS = 2048
CAP = 36
N_SECTION = 2
N_EXPERT = 16


def levels(key, dims, pieces, smallest, top_value):
    loudness = 1.0
    for axis_at, parts in pieces:
        heights = jax.random.uniform(jax.random.fold_in(jax.random.fold_in(key, 6), axis_at), (parts,), jnp.float32, smallest / len(pieces), top_value / len(pieces))
        loudness = loudness * jnp.repeat(jnp.exp(heights), dims[axis_at] // parts).reshape((-1,) + (1,) * (len(dims) - 1 - axis_at))
    return loudness


def assign_block(key, own, number, rows, count, top, reach, skew):
    order = jax.random.permutation(key, count)
    heavy_load, ordinary = shares(count, rows * top, reach, skew, True), shares(count, rows * top, reach, skew, False)
    places = jnp.arange(count)

    def named(sizes, offset_by):
        used = int((sizes > 0).sum())
        fixed = max(1, used // 4)
        shifted = fixed + (places - fixed + offset_by * (used - fixed)) % max(1, count - fixed)
        return jnp.zeros((count,), jnp.int32).at[order[jnp.where(places < fixed, places, shifted)]].set(jnp.asarray(sizes, jnp.int32))

    sizes = jnp.where(number % 4 == 0, named(heavy_load, number // 4), named(ordinary, number - number // 4 - 1))
    mixed = jax.random.permutation(jax.random.fold_in(own, 3), count)
    giver, sink = mixed[0:count // 2 * 2:2], mixed[1:count // 2 * 2:2]
    room = jnp.minimum(sizes[giver] - 1, reach - sizes[sink]) // 2
    room = jnp.where((giver == order[0]) | (sink == order[0]) | (sizes[sink] == 0), 0, jnp.maximum(room, 0))
    shifted = jax.random.randint(jax.random.fold_in(own, 4), (count // 2,), 0, 1 << 20) % (room + 1)
    sizes = sizes.at[giver].add(-shifted).at[sink].add(shifted)
    members = jnp.searchsorted(jnp.cumsum(sizes), jnp.arange(rows * top), side="right").astype(jnp.int32)
    grid = members.reshape(top, rows).T
    grid = grid[jax.random.permutation(jax.random.fold_in(own, 1), rows)]
    offset_by = jax.random.randint(jax.random.fold_in(own, 2), (rows, 1), 0, top)
    return jnp.take_along_axis(grid, (jnp.arange(top)[None, :] + offset_by) % top, axis=1)


def shares(number_of, total, reach, skew, full):
    loads = [(1 << 20) // math.isqrt(standing ** skew) + 1 for standing in range(1, number_of + 1)]
    largest = reach if full else min(reach, max(-(-total // number_of), total * loads[0] // sum(loads)))
    least = 1 if total - largest >= number_of - 1 else 0
    given, spare = [largest] + [least] * (number_of - 1), total - largest - least * (number_of - 1)
    while spare > 0:
        movable = [i for i in range(1, number_of) if given[i] < largest] or [i for i in range(1, number_of) if given[i] < reach]
        pool, remaining = sum([loads[i] for i in movable]), spare
        for i in movable:
            addition = min(reach - given[i], max(1, remaining * loads[i] // pool), spare)
            given[i] = given[i] + addition
            spare = spare - addition
    return np.array(given)


def centred(own_key, dims, width, limit, pieces=(), held_as=jnp.bfloat16):
    factor_of = levels(own_key, dims, pieces, -0.22, 0.18) if pieces else 1.0
    values = jax.random.normal(own_key, dims, jnp.float32) * width * factor_of
    return jnp.minimum(jnp.maximum(values, -limit), limit).astype(held_as)


def setup_inputs(seed: int = 0) -> dict:
    streams_of = jax.random.split(jax.random.key(seed), 8)
    tokens = centred(streams_of[0], (TOKENS, D), 1.0, 6.0, ((0, 16),))
    norm_gain = jnp.clip(1.0 + 0.15 * jax.random.normal(streams_of[1], (D,), jnp.float32), 0.25, 1.75).astype(jnp.bfloat16)
    router = centred(streams_of[2], (D, EXPERTS), D ** -0.5, 0.09375)
    w_gate = centred(streams_of[3], (EXPERTS, D, FF), D ** -0.5, 0.09375, ((0, 16), (2, 2)))
    w_up = centred(streams_of[4], (EXPERTS, D, FF), D ** -0.5, 0.09375, ((0, 16), (2, 2)))
    w_down = centred(streams_of[5], (EXPERTS, FF, D), FF ** -0.5, 0.1875, ((0, 16), (1, 2)))
    expert_ids_keys = jax.random.split(jax.random.fold_in(streams_of[6], 1), TOKENS // TOK_DEV)
    expert_ids_turns = jax.random.permutation(jax.random.fold_in(streams_of[6], 3), TOKENS // TOK_DEV)
    expert_ids = jax.vmap(lambda own, number: assign_block(jax.random.fold_in(streams_of[6], 2), own, number, TOK_DEV, EXPERTS, TOP, CAP, 2))(expert_ids_keys, expert_ids_turns).reshape((TOKENS, TOP))
    return {"tokens": tokens, "norm_gain": norm_gain, "router": router, "w_gate": w_gate, "w_up": w_up, "w_down": w_down, "expert_ids": expert_ids}


EPSILON = 1e-06

def reference(tokens, norm_gain, router, w_gate, w_up, w_down, expert_ids):
    tokens_f = tokens.astype(jnp.float32)
    mean_sq = lax.optimization_barrier(jnp.mean(tokens_f * tokens_f, axis=-1, keepdims=True))
    normed = (tokens_f * lax.rsqrt(mean_sq + EPSILON) * norm_gain.astype(jnp.float32)).astype(jnp.bfloat16)
    logits = jnp.dot(normed, router, preferred_element_type=jnp.float32)
    scores = jax.nn.sigmoid(logits)
    picked = jnp.take_along_axis(scores, expert_ids, axis=1)
    route_weight = 2.5 * picked / lax.optimization_barrier(jnp.sum(picked, axis=1, keepdims=True))
    blocks = N_EXPERT
    tok_block = TOK_DEV
    ids_block = expert_ids.reshape(blocks, tok_block * TOP)
    onehot = (ids_block[:, :, None] == jnp.arange(EXPERTS, dtype=jnp.int32)[None, None, :]).astype(jnp.int32)
    before = jnp.cumsum(onehot, axis=1) - onehot
    slot_rank = lax.optimization_barrier(jnp.sum(onehot * before, axis=-1)).astype(jnp.int32)
    block_ids = jnp.broadcast_to(jnp.arange(blocks, dtype=jnp.int32)[:, None], (blocks, tok_block * TOP))
    row_index = block_ids * tok_block + (jnp.arange(tok_block * TOP, dtype=jnp.int32) // TOP)[None, :]
    row_table = jnp.full((EXPERTS, blocks, CAP), TOKENS, jnp.int32).at[ids_block, block_ids, slot_rank].set(row_index)
    gate_table = jnp.zeros((EXPERTS, blocks, CAP), jnp.float32).at[ids_block, block_ids, slot_rank].set(route_weight.reshape(blocks, tok_block * TOP))
    padded = jnp.concatenate([normed, jnp.zeros((1, D), jnp.bfloat16)], axis=0)
    hid_width = FF // N_SECTION

    def add_expert(totals, expert):
        gather_rows = row_table[expert].reshape(-1)
        inputs = padded[gather_rows]
        gate_act = jnp.dot(inputs, w_gate[expert], preferred_element_type=jnp.float32)
        up_act = jnp.dot(inputs, w_up[expert], preferred_element_type=jnp.float32)
        hidden = (jax.nn.silu(gate_act) * up_act).astype(jnp.bfloat16)
        down = w_down[expert]
        output_sum = jnp.zeros((gather_rows.shape[0], D), jnp.float32)
        for section in range(N_SECTION):
            partial_value = jnp.dot(hidden[:, section * hid_width:(section + 1) * hid_width], down[section * hid_width:(section + 1) * hid_width], preferred_element_type=jnp.float32).astype(jnp.bfloat16)
            output_sum = output_sum + partial_value.astype(jnp.float32)
        weighted = gate_table[expert].reshape(-1)[:, None] * output_sum
        return (totals.at[gather_rows].add(weighted), None)
    totals, _ = lax.scan(add_expert, jnp.zeros((TOKENS + 1, D), jnp.float32), jnp.arange(EXPERTS, dtype=jnp.int32))
    return (tokens_f + totals[:TOKENS]).astype(jnp.bfloat16)
```

```python
import jax
import jax.numpy as jnp
from jax import lax
from jax.sharding import PartitionSpec as P

EPSILON = 1e-06
F32, BF16 = jnp.float32, jnp.bfloat16


def per_device(sections, experts, tokens, norm_gain, router, w_gate, w_up, w_down, expert_ids):
    tok_count, model_width = tokens.shape
    top_count = expert_ids.shape[1]
    cap = tok_count * top_count * 3 // (2 * experts)
    width = model_width // sections
    half = experts // 2
    chips = experts // 4
    me = lax.axis_index("expert")
    section = lax.axis_index("section")

    def swap(value, mask):
        return lax.ppermute(value, "expert", [(i, i ^ mask) for i in range(experts)])

    tokens_f = tokens.astype(F32)
    mean_sq = jnp.mean(tokens_f * tokens_f, axis=-1, keepdims=True)
    normed = (tokens_f * lax.rsqrt(mean_sq + EPSILON) * norm_gain.astype(F32)).astype(BF16)
    mine = lax.dynamic_slice_in_dim(normed, section * width, width, 1)

    def table(ids):
        named = jnp.any(ids[:, :, None] == jnp.arange(experts, dtype=jnp.int32), axis=1)
        rows = lax.broadcasted_iota(jnp.int32, (tok_count, tok_count), 0)
        cols = lax.broadcasted_iota(jnp.int32, (tok_count, tok_count), 1)
        before = jnp.dot(
            (cols < rows).astype(BF16), named.astype(BF16), preferred_element_type=F32
        )
        return named, jnp.where(named, before, -1.0)

    ids_core = swap(expert_ids, 1)
    ids_far = swap(expert_ids, half)
    ids_far_core = swap(expert_ids, half + 1)
    named, table_own = table(expert_ids)
    logits = jnp.dot(normed, router, preferred_element_type=F32)
    scores = jnp.where(named, jax.nn.sigmoid(logits), 0.0)
    weight = 2.5 * scores / jnp.sum(scores, axis=1, keepdims=True)
    weight_core = swap(weight, 1)
    weight_far = swap(weight, half)
    weight_far_core = swap(weight, half + 1)

    near = (((me // 2) ^ jnp.arange(chips, dtype=jnp.int32)) * 2 + me % 2)[:, None]
    near = (near == jnp.arange(experts, dtype=jnp.int32)[None, :]).astype(F32)

    def columns(first, second):
        both = jnp.concatenate([first, second], axis=0)
        return lax.dot_general(
            near, both, (((1,), (1,)), ((), ())), precision=lax.Precision.HIGHEST,
            preferred_element_type=F32,
        )

    row = lax.broadcasted_iota(jnp.int32, (1, 2 * cap, 2 * tok_count), 1)
    col = lax.broadcasted_iota(jnp.int32, (1, 2 * cap, 2 * tok_count), 2)
    wanted = jnp.where(row // cap == col // tok_count, row % cap, -2).astype(F32)

    def choose(first, second):
        return columns(first, second)[:, None, :] == wanted

    def pick(chosen, toks):
        flat = chosen.astype(BF16).reshape(chips * 2 * cap, 2 * tok_count)
        return jnp.dot(flat, toks, preferred_element_type=F32).astype(BF16).reshape(
            chips, 2 * cap, toks.shape[1]
        )

    def spread(rows):
        return jnp.concatenate(
            [rows[:1]] + [swap(rows[q : q + 1], 2 * q) for q in range(1, chips)], axis=0
        )

    def feature_exchange(rows):
        rows = rows.reshape(chips * 2 * cap, rows.shape[2])
        if sections == 2:
            other = lax.ppermute(rows, "section", [(0, 1), (1, 0)])
            low = jnp.where(section == 0, rows, other)
            high = jnp.where(section == 0, other, rows)
            return jnp.concatenate([low, high], axis=1)
        return lax.all_gather(rows, "section", axis=1, tiled=True)

    def experts_of(full):
        gate_act = jnp.dot(full, w_gate[0], preferred_element_type=F32)
        up_act = jnp.dot(full, w_up[0], preferred_element_type=F32)
        hidden = (jax.nn.silu(gate_act) * up_act).astype(BF16)
        part = jnp.dot(hidden, w_down[0], preferred_element_type=F32).astype(BF16)
        if sections == 2:
            keep = lax.dynamic_slice_in_dim(part, section * width, width, 1)
            give = lax.dynamic_slice_in_dim(part, (1 - section) * width, width, 1)
            got = lax.ppermute(give, "section", [(0, 1), (1, 0)])
            done = (keep.astype(F32) + got.astype(F32)).astype(BF16)
        else:
            done = lax.psum_scatter(part, "section", scatter_dimension=1, tiled=True)
        return done.reshape(chips, 2 * cap, width)

    def mix(chosen, first, second, rows):
        factors = jnp.where(chosen, columns(first, second)[:, None, :], 0.0).astype(BF16)
        factors = factors.reshape(chips * 2 * cap, 2 * tok_count)
        both = lax.dot_general(
            factors, rows.reshape(chips * 2 * cap, width), (((0,), (0,)), ((), ())),
            preferred_element_type=F32,
        )
        got = swap(both[tok_count:].astype(BF16), 1)
        return both[:tok_count] + got.astype(F32)

    chosen_near = choose(table_own, table(ids_core)[1])
    toks_near = jnp.concatenate([mine, swap(mine, 1)], axis=0)
    full_near = feature_exchange(spread(pick(chosen_near, toks_near)))
    far = swap(mine, half)
    chosen_far = choose(table(ids_far)[1], table(ids_far_core)[1])
    toks_far = jnp.concatenate([far, swap(far, 1)], axis=0)
    full_far = feature_exchange(spread(pick(chosen_far, toks_far)))

    back_near = spread(experts_of(full_near))
    back_far = spread(experts_of(full_far))
    sum_far = swap(mix(chosen_far, weight_far, weight_far_core, back_far).astype(BF16), half)
    sum_near = mix(chosen_near, weight, weight_core, back_near)
    residual = lax.dynamic_slice_in_dim(tokens, section * width, width, 1)
    return (residual.astype(F32) + sum_near + sum_far.astype(F32)).astype(BF16)


def solution(mesh):
    placed = (
        P("expert", None),
        P(),
        P(),
        P("expert", None, "section"),
        P("expert", None, "section"),
        P("expert", "section", None),
        P("expert", None),
    )

    def body(*args):
        return per_device(mesh.shape["section"], mesh.shape["expert"], *args)

    return jax.shard_map(
        body, mesh=mesh, in_specs=placed, out_specs=P("expert", "section"), check_vma=False
    )
```

```python
import functools

import jax
import jax.numpy as jnp
from jax import lax
from jax.experimental import pallas as pl
from jax.experimental.pallas import tpu as pltpu
from jax.sharding import PartitionSpec as P

EPSILON = 1e-06
F32, BF16 = jnp.float32, jnp.bfloat16


def any_sections(sections, experts, tokens, norm_gain, router, w_gate, w_up, w_down, expert_ids):
    tok_count, model_width = tokens.shape
    top_count = expert_ids.shape[1]
    cap = tok_count * top_count * 3 // (2 * experts)
    width = model_width // sections
    half = experts // 2
    chips = experts // 4
    me = lax.axis_index("expert")
    section = lax.axis_index("section")

    def swap(value, mask):
        return lax.ppermute(value, "expert", [(i, i ^ mask) for i in range(experts)])

    tokens_f = tokens.astype(F32)
    mean_sq = jnp.mean(tokens_f * tokens_f, axis=-1, keepdims=True)
    normed = (tokens_f * lax.rsqrt(mean_sq + EPSILON) * norm_gain.astype(F32)).astype(BF16)
    mine = lax.dynamic_slice_in_dim(normed, section * width, width, 1)

    def table(ids):
        named = jnp.any(ids[:, :, None] == jnp.arange(experts, dtype=jnp.int32), axis=1)
        rows = lax.broadcasted_iota(jnp.int32, (tok_count, tok_count), 0)
        cols = lax.broadcasted_iota(jnp.int32, (tok_count, tok_count), 1)
        before = jnp.dot(
            (cols < rows).astype(BF16), named.astype(BF16), preferred_element_type=F32
        )
        return named, jnp.where(named, before, -1.0)

    ids_core = swap(expert_ids, 1)
    ids_far = swap(expert_ids, half)
    ids_far_core = swap(expert_ids, half + 1)
    named, table_own = table(expert_ids)
    logits = jnp.dot(normed, router, preferred_element_type=F32)
    scores = jnp.where(named, jax.nn.sigmoid(logits), 0.0)
    weight = 2.5 * scores / jnp.sum(scores, axis=1, keepdims=True)
    weight_core = swap(weight, 1)
    weight_far = swap(weight, half)
    weight_far_core = swap(weight, half + 1)

    near = (((me // 2) ^ jnp.arange(chips, dtype=jnp.int32)) * 2 + me % 2)[:, None]
    near = (near == jnp.arange(experts, dtype=jnp.int32)[None, :]).astype(F32)

    def columns(first, second):
        both = jnp.concatenate([first, second], axis=0)
        return lax.dot_general(
            near, both, (((1,), (1,)), ((), ())), precision=lax.Precision.HIGHEST,
            preferred_element_type=F32,
        )

    row = lax.broadcasted_iota(jnp.int32, (1, 2 * cap, 2 * tok_count), 1)
    col = lax.broadcasted_iota(jnp.int32, (1, 2 * cap, 2 * tok_count), 2)
    wanted = jnp.where(row // cap == col // tok_count, row % cap, -2).astype(F32)

    def choose(first, second):
        return columns(first, second)[:, None, :] == wanted

    def pick(chosen, toks):
        flat = chosen.astype(BF16).reshape(chips * 2 * cap, 2 * tok_count)
        return jnp.dot(flat, toks, preferred_element_type=F32).astype(BF16).reshape(
            chips, 2 * cap, toks.shape[1]
        )

    def spread(rows):
        return jnp.concatenate(
            [rows[:1]] + [swap(rows[q : q + 1], 2 * q) for q in range(1, chips)], axis=0
        )

    def feature_exchange(rows):
        rows = rows.reshape(chips * 2 * cap, rows.shape[2])
        if sections == 2:
            other = lax.ppermute(rows, "section", [(0, 1), (1, 0)])
            low = jnp.where(section == 0, rows, other)
            high = jnp.where(section == 0, other, rows)
            return jnp.concatenate([low, high], axis=1)
        return lax.all_gather(rows, "section", axis=1, tiled=True)

    def experts_of(full):
        gate_act = jnp.dot(full, w_gate[0], preferred_element_type=F32)
        up_act = jnp.dot(full, w_up[0], preferred_element_type=F32)
        hidden = (jax.nn.silu(gate_act) * up_act).astype(BF16)
        part = jnp.dot(hidden, w_down[0], preferred_element_type=F32).astype(BF16)
        if sections == 2:
            keep = lax.dynamic_slice_in_dim(part, section * width, width, 1)
            give = lax.dynamic_slice_in_dim(part, (1 - section) * width, width, 1)
            got = lax.ppermute(give, "section", [(0, 1), (1, 0)])
            done = (keep.astype(F32) + got.astype(F32)).astype(BF16)
        else:
            done = lax.psum_scatter(part, "section", scatter_dimension=1, tiled=True)
        return done.reshape(chips, 2 * cap, width)

    def mix(chosen, first, second, rows):
        factors = jnp.where(chosen, columns(first, second)[:, None, :], 0.0).astype(BF16)
        factors = factors.reshape(chips * 2 * cap, 2 * tok_count)
        both = lax.dot_general(
            factors, rows.reshape(chips * 2 * cap, width), (((0,), (0,)), ((), ())),
            preferred_element_type=F32,
        )
        got = swap(both[tok_count:].astype(BF16), 1)
        return both[:tok_count] + got.astype(F32)

    chosen_near = choose(table_own, table(ids_core)[1])
    toks_near = jnp.concatenate([mine, swap(mine, 1)], axis=0)
    full_near = feature_exchange(spread(pick(chosen_near, toks_near)))
    far = swap(mine, half)
    chosen_far = choose(table(ids_far)[1], table(ids_far_core)[1])
    toks_far = jnp.concatenate([far, swap(far, 1)], axis=0)
    full_far = feature_exchange(spread(pick(chosen_far, toks_far)))

    back_near = spread(experts_of(full_near))
    back_far = spread(experts_of(full_far))
    sum_far = swap(mix(chosen_far, weight_far, weight_far_core, back_far).astype(BF16), half)
    sum_near = mix(chosen_near, weight, weight_core, back_near)
    residual = lax.dynamic_slice_in_dim(tokens, section * width, width, 1)
    return (residual.astype(F32) + sum_near + sum_far.astype(F32)).astype(BF16)


def prepare_body(experts, place, *refs):
    out, first, second = refs[4:7]
    tokens, gain, router, ids, sems = refs[7:]
    copies = [
        pltpu.make_async_copy(source, target, sems.at[i])
        for i, (source, target) in enumerate(zip(refs[:4], refs[7:11]))
    ]
    for copy in copies:
        copy.start()
    for copy in copies:
        copy.wait()
    tok_count, model_width = tokens.shape
    width = model_width // 2
    tokens_f = tokens[...].astype(F32)
    mean_sq = jnp.mean(tokens_f * tokens_f, axis=-1, keepdims=True)
    gain_f = gain[...].reshape(1, model_width).astype(F32)
    normed = (tokens_f * lax.rsqrt(mean_sq + EPSILON) * gain_f).astype(BF16)
    by_feature = (((1,), (1,)), ((), ()))
    logits = lax.dot_general(router[...], normed, by_feature, preferred_element_type=F32)
    expert = lax.broadcasted_iota(jnp.int32, (experts, tok_count), 0)
    named = ids[0:1, :] == expert
    for k in range(1, ids.shape[0]):
        named = named | (ids[k : k + 1, :] == expert)
    rows = lax.broadcasted_iota(jnp.int32, (tok_count, tok_count), 0)
    cols = lax.broadcasted_iota(jnp.int32, (tok_count, tok_count), 1)
    before = jnp.dot(
        named.astype(F32).astype(BF16),
        (rows < cols).astype(F32).astype(BF16),
        preferred_element_type=F32,
    )
    slot = jnp.where(named, before, -1.0)
    scores = jnp.where(named, 1.0 / (1.0 + jnp.exp(-logits)), 0.0)
    weight = 2.5 * scores / jnp.sum(scores, axis=0, keepdims=True)
    meta = jnp.concatenate(
        [slot, weight, jnp.zeros((128 - 2 * experts, tok_count), F32)], axis=0
    ).astype(BF16)
    meta = lax.dot_general(
        (rows == cols).astype(F32).astype(BF16), meta, by_feature, preferred_element_type=F32
    )
    meta = meta.astype(BF16)
    swapped = place[0] == 1
    low, high = normed[:, :width], normed[:, width:]
    mine = jnp.where(swapped, high, low)
    out[:, :width] = mine
    out[:, width:model_width] = jnp.where(swapped, low, high)
    out[:, model_width:] = meta
    first[:, : width // 2] = mine[:, : width // 2]
    first[:, width // 2 :] = meta
    second[...] = mine[:, width // 2 :]


def prepare(experts, place, tokens, norm_gain, router, expert_ids):
    tok_count, model_width = tokens.shape
    arrays = (tokens, norm_gain, router.T, expert_ids.T)
    return pl.pallas_call(
        functools.partial(prepare_body, experts),
        out_shape=[
            jax.ShapeDtypeStruct((tok_count, columns), BF16)
            for columns in (model_width + 128, model_width // 4 + 128, model_width // 4)
        ],
        in_specs=[pl.BlockSpec(memory_space=pltpu.SMEM)] + [pl.BlockSpec(memory_space=pl.ANY)] * 4,
        out_specs=[pl.BlockSpec(memory_space=pltpu.VMEM)] * 3,
        scratch_shapes=[pltpu.VMEM(a.shape, a.dtype) for a in arrays]
        + [pltpu.SemaphoreType.DMA((4,))],
        compiler_params=pltpu.CompilerParams(vmem_limit_bytes=60 * 1024 * 1024),
        name="prepare",
    )(place, *arrays)


def mlp_body(plan, steps, carried, outs, cap, place, *refs):
    count = 1 + max(piece for _, where in plan for piece, _ in where.values())
    pieces, (w_gate, w_up, w_down) = refs[:count], refs[count : count + 3]
    refs = refs[count + 3 :]
    before = refs[:2] if carried else ()
    refs = refs[2:] if carried else refs
    results, (gate_w, up_w, down_w, in_sems, down_sems) = refs[:-5], refs[-5:]
    model_width, hidden_width = w_gate.shape[1], w_gate.shape[2]
    step = gate_w.shape[1]
    total = model_width // step

    def start_of(number):
        side, index = number // (total // 2), number % (total // 2)
        return pl.multiple_of(jnp.where(place[0] == side, 0, model_width // 2) + index * step, step)

    def load(at, number):
        rows = pl.ds(start_of(number), step)
        return (
            pltpu.make_async_copy(w_gate.at[0, rows, :], gate_w.at[at], in_sems.at[0, at]),
            pltpu.make_async_copy(w_up.at[0, rows, :], up_w.at[at], in_sems.at[1, at]),
        )

    def load_down(number):
        return pltpu.make_async_copy(
            w_down.at[0, :, pl.ds(start_of(number), step)], down_w.at[number], down_sems.at[number]
        )

    order = (2, 0, 1, 3)
    for at, number in enumerate(steps):
        for copy in load(at, number):
            copy.start()
    for number in order if outs else ():
        load_down(number).start()
    gates, ups = [], []
    first = 0
    for rows, _ in plan:
        for sums, ref in zip((gates, ups), before or (None, None)):
            zero = jnp.zeros((rows, hidden_width), F32)
            sums.append(zero if ref is None else ref[first : first + rows, :])
        first += rows
    for at, number in enumerate(steps):
        for copy in load(at, number):
            copy.wait()
        for b, (_, where) in enumerate(plan):
            piece, column = where[number]
            x = pieces[piece][:, column : column + step]
            gates[b] += jnp.dot(x, gate_w[at], preferred_element_type=F32)
            ups[b] += jnp.dot(x, up_w[at], preferred_element_type=F32)
    if not outs:
        first = 0
        for gate, up in zip(gates, ups):
            for ref, value in zip(results, (gate, up)):
                ref[first : first + value.shape[0], :] = value
            first += gate.shape[0]
        return
    hidden = [(g / (1.0 + jnp.exp(-g)) * u).astype(BF16) for g, u in zip(gates, ups)]
    if cap:
        rows = plan[0][0]
        to = lax.broadcasted_iota(jnp.int32, (rows, rows), 0)
        of = lax.broadcasted_iota(jnp.int32, (rows, rows), 1)
        spot = to % (rows // 2)
        moved = spot // cap * 2 * cap + to // (rows // 2) * cap + spot % cap == of
        hidden = [
            jnp.dot(
                moved.astype(F32).astype(BF16), hidden[0], preferred_element_type=F32
            ).astype(BF16)
        ]
    for number in order:
        load_down(number).wait()
        first = 0
        for h in hidden:
            y = jnp.dot(h, down_w[number], preferred_element_type=F32).astype(BF16)
            for (start, rows, covers), ref in zip(outs, results):
                low, high = max(start, first), min(start + rows, first + h.shape[0])
                if number in covers and low < high:
                    at = covers.index(number) * step
                    ref[low - start : high - start, at : at + step] = y[low - first : high - first]
            first += h.shape[0]


def mlp(place, blocks, steps, before, w_gate, w_up, w_down, outs, cap=0):
    _, model_width, hidden_width = w_gate.shape
    total = 4
    step = model_width // total
    plan, pieces = [], []
    for block in blocks:
        where = {}
        for piece, covers in block:
            for at, number in enumerate(covers):
                where[number] = (len(pieces), at * step)
            pieces.append(piece)
        plan.append((block[0][0].shape[0], where))
    rows = sum(r for r, _ in plan)
    vmem = pl.BlockSpec(memory_space=pltpu.VMEM)
    if outs:
        shapes = [jax.ShapeDtypeStruct((r, len(c) * step), BF16) for _, r, c in outs]
    else:
        shapes = [jax.ShapeDtypeStruct((rows, hidden_width), F32)] * 2
    return pl.pallas_call(
        functools.partial(mlp_body, plan, steps, bool(before), outs, cap),
        out_shape=shapes,
        in_specs=[pl.BlockSpec(memory_space=pltpu.SMEM)]
        + [vmem] * len(pieces)
        + [pl.BlockSpec(memory_space=pl.ANY)] * 3
        + [vmem] * len(before),
        out_specs=[vmem] * len(shapes),
        scratch_shapes=[
            pltpu.VMEM((len(steps), step, hidden_width), BF16),
            pltpu.VMEM((len(steps), step, hidden_width), BF16),
            pltpu.VMEM((total if outs else 1, hidden_width, step), BF16),
            pltpu.SemaphoreType.DMA((2, len(steps))),
            pltpu.SemaphoreType.DMA((total,)),
        ],
        compiler_params=pltpu.CompilerParams(vmem_limit_bytes=40 * 1024 * 1024),
        cost_estimate=pl.CostEstimate(
            flops=4 * rows * step * len(steps) * hidden_width
            + (2 * rows * model_width * hidden_width if outs else 0),
            bytes_accessed=4 * step * len(steps) * hidden_width
            + (2 * model_width * hidden_width if outs else 0),
            transcendentals=rows * hidden_width if outs else 0,
        ),
        name="mlp",
    )(place, *pieces, w_gate, w_up, w_down, *before)


def join_body(cap, column, keep, crossed, beside, slanted, *outs):
    rows, width = keep.shape
    first = (keep[...].astype(F32) + crossed[...].astype(F32)).astype(BF16)
    second = beside[:, column : column + width].astype(F32) + slanted[...].astype(F32)
    second = second.astype(BF16)
    to = lax.broadcasted_iota(jnp.int32, (2 * cap, rows), 0)
    of = lax.broadcasted_iota(jnp.int32, (2 * cap, rows), 1)
    for q, out in enumerate(outs):
        here = (q * cap + to % cap == of).astype(F32)
        out[...] = (
            jnp.dot(jnp.where(to < cap, here, 0.0).astype(BF16), first, preferred_element_type=F32)
            + jnp.dot(jnp.where(to < cap, 0.0, here).astype(BF16), second, preferred_element_type=F32)
        ).astype(BF16)


def join(cap, chips, column, keep, crossed, beside, slanted):
    vmem = pl.BlockSpec(memory_space=pltpu.VMEM)
    return pl.pallas_call(
        functools.partial(join_body, cap, column),
        out_shape=[jax.ShapeDtypeStruct((2 * cap, keep.shape[1]), BF16)] * chips,
        in_specs=[vmem] * 4,
        out_specs=[vmem] * chips,
        compiler_params=pltpu.CompilerParams(vmem_limit_bytes=32 * 1024 * 1024),
        name="join",
    )(keep, crossed, beside, slanted)


def two_sections(experts, tokens, norm_gain, router, w_gate, w_up, w_down, expert_ids):
    tok_count, model_width = tokens.shape
    top_count = expert_ids.shape[1]
    cap = tok_count * top_count * 3 // (2 * experts)
    width = model_width // 2
    half = experts // 2
    chips = experts // 4
    me = lax.axis_index("expert")
    section = lax.axis_index("section")
    place = jnp.reshape(section, (1,)).astype(jnp.int32)
    group = 2 * cap

    def swap(value, mask):
        return lax.ppermute(value, "expert", [(i, i ^ mask) for i in range(experts)])

    def cross(value):
        return lax.ppermute(value, "section", [(0, 1), (1, 0)])

    def slant(value):
        pairs = [(s * experts + i, (1 - s) * experts + (i ^ 1)) for s in (0, 1) for i in range(experts)]
        return lax.ppermute(value, ("section", "expert"), pairs)

    packed, mine_0, mine_1 = prepare(experts, place, tokens, norm_gain, router, expert_ids)
    beside = swap(packed, 1)

    near = (((me // 2) ^ jnp.arange(chips, dtype=jnp.int32)) * 2 + me % 2)[:, None]
    lanes = jnp.arange(128, dtype=jnp.int32)[None, :]
    near = jnp.concatenate([near == lanes, near + experts == lanes], axis=0).astype(BF16)
    row = lax.broadcasted_iota(jnp.int32, (1, group, 2 * tok_count), 1)
    col = lax.broadcasted_iota(jnp.int32, (1, group, 2 * tok_count), 2)
    wanted = jnp.where(row // cap == col // tok_count, row % cap, -2).astype(F32)

    def tables(first, second):
        found = jnp.concatenate(
            [
                lax.dot_general(near, m, (((1,), (1,)), ((), ())), preferred_element_type=F32)
                for m in (first, second)
            ],
            axis=1,
        )
        chosen = found[:chips, None, :] == wanted
        factors = jnp.where(chosen, found[chips:, None, :], 0.0).astype(BF16)
        return chosen.astype(BF16), factors.reshape(chips * group, 2 * tok_count)

    def pick(chosen, first, second):
        flat = chosen.reshape(-1, 2 * tok_count)
        return (
            jnp.dot(flat[:, :tok_count], first, preferred_element_type=F32)
            + jnp.dot(flat[:, tok_count:], second, preferred_element_type=F32)
        ).astype(BF16)

    def pieces_of(rows, number):
        return [rows[q * group : (q + 1) * group] for q in range(number)]

    def spread(pieces):
        return [swap(piece, 2 * q) if q else piece for q, piece in enumerate(pieces)]

    def mix(factors, rows):
        return lax.dot_general(
            factors, rows, (((0,), (0,)), ((), ())), preferred_element_type=F32
        )

    def stage(*values):
        return lax.optimization_barrier(values)

    def core_sum(mixed):
        got = swap(mixed[tok_count:].astype(BF16), 1)
        return mixed[:tok_count], got

    def both_factors(block):
        number = jnp.arange(2 * chips, dtype=jnp.int32)
        number = (((me // 2) ^ (number // 2)) * 2 + (me % 2 ^ number % 2))[:, None]
        at = jnp.concatenate([number == lanes, number + experts == lanes], axis=0).astype(BF16)
        found = lax.dot_general(at, block, (((1,), (1,)), ((), ())), preferred_element_type=F32)
        found = found.reshape(2, chips, 2, 1, tok_count)
        line = lax.broadcasted_iota(jnp.int32, (1, group, tok_count), 1)
        slot, weight = jnp.where(line < cap, found[:, :, 0], found[:, :, 1])
        chosen = slot == (line % cap).astype(F32)
        return jnp.where(chosen, weight, 0.0).astype(BF16).reshape(chips * group, tok_count)

    weights = (w_gate, w_up, w_down)
    part = width // 2
    meta = packed[:, model_width:]
    far_0 = swap(mine_0, half)

    chosen, factors = tables(meta, beside[:, model_width:])
    some = pieces_of(pick(chosen[2:], packed[:, :width], beside[:, :width]), chips - 2)
    whole = pick(chosen[:2], packed[:, :model_width], beside[:, :model_width])
    some = [swap(piece, 2 * q) for q, piece in enumerate(some, 2)]
    whole_near = swap(whole[group:], 2)
    some, whole_0, whole_near, far_0, mine_1 = stage(some, whole[:group], whole_near, far_0, mine_1)

    some = jnp.concatenate(some, axis=0)
    some_other = cross(some)
    far_1 = swap(mine_1, half)
    beside_0 = swap(far_0, 1)
    far_chosen, _ = tables(far_0[:, part:], beside_0[:, part:])
    rows_0 = spread(pieces_of(pick(far_chosen, far_0[:, :part], beside_0[:, :part]), chips))
    some, rows_0, far_1 = stage(some, rows_0, far_1)

    rows_0 = jnp.concatenate(rows_0, axis=0)
    other_0 = cross(rows_0)
    rows_1 = spread(pieces_of(pick(far_chosen, far_1, swap(far_1, 1)), chips))
    whole = jnp.concatenate([whole_0, whole_near], axis=0)
    all_rows = chips * group
    (near,) = mlp(
        place, [[(whole, (0, 1, 2, 3))], [(some, (0, 1)), (some_other, (2, 3))]],
        (0, 1, 2, 3), (), *weights, [(0, all_rows, (0, 1, 2, 3))],
    )
    rows_0, rows_1, near = stage(rows_0, rows_1, near)

    rows_1 = jnp.concatenate(rows_1, axis=0)
    other_1 = cross(rows_1)
    near = pieces_of(near, chips)
    near_back = near[:1] + [swap(near[q], 2 * q) for q in range(1, chips - 1)]
    sums = mlp(
        place, [[(rows_0, (0,)), (rows_1, (1,)), (other_0, (2,))]], (0, 1, 2), (), *weights, ()
    )
    other_1, near_back, near_last, sums = stage(other_1, near_back, near[-1], sums)

    side = all_rows // 2
    outs = mlp(
        place, [[(other_1, (3,))]], (3,), sums, *weights,
        [(first, side, (k,)) for k in (2, 0, 1, 3) for first in (0, side)], cap,
    )
    (give_0, slant_0, keep_0, core_0, keep_1, core_1, give_1, slant_1), near_last = stage(outs, near_last)
    got_0 = cross(give_0)
    slant_0 = slant(slant_0)
    core_0 = swap(core_0, 1)
    near_last = swap(near_last, 2 * (chips - 1))
    got_1 = cross(give_1)
    slant_1 = slant(slant_1)
    got_0, slant_0, core_0, near_last, core_1, near_back = stage(
        got_0, slant_0, core_0, near_last, core_1, near_back
    )

    core_1 = swap(core_1, 1)
    back_0 = spread(join(cap, chips, 0, keep_0, got_0, core_0, slant_0))
    near_sum = mix(factors, jnp.concatenate(near_back + [near_last], axis=0))
    got_1, slant_1, core_1, back_0, near_sum = stage(got_1, slant_1, core_1, back_0, near_sum)

    far_factors = both_factors(far_0[:, part:])
    far_0 = swap(mix(far_factors, jnp.concatenate(back_0, axis=0)).astype(BF16), half)
    back_1 = spread(join(cap, chips, 0, keep_1, got_1, core_1, slant_1))
    near_sum, near_core = core_sum(near_sum)
    near_sum, near_core, far_0, back_1 = stage(near_sum, near_core, far_0, back_1)

    far_1 = swap(mix(far_factors, jnp.concatenate(back_1, axis=0)).astype(BF16), half)
    near_sum = near_sum + near_core.astype(F32)
    near_got = cross(near_sum[:, width:].astype(BF16))
    far_sum = jnp.concatenate([far_0, far_1], axis=1).astype(F32)
    residual = lax.dynamic_slice_in_dim(tokens, section * width, width, 1)
    return (residual.astype(F32) + near_sum[:, :width] + near_got.astype(F32) + far_sum).astype(BF16)


def solution(mesh):
    placed = (
        P("expert", None),
        P(),
        P(),
        P("expert", None, "section"),
        P("expert", None, "section"),
        P("expert", "section", None),
        P("expert", None),
    )

    def body(*args):
        sections, experts = mesh.shape["section"], mesh.shape["expert"]
        if sections == 2 and experts <= 64:
            return two_sections(experts, *args)
        return any_sections(sections, experts, *args)

    return jax.shard_map(
        body, mesh=mesh, in_specs=placed, out_specs=P("expert", "section"), check_vma=False
    )
```

```python
import functools

import jax
import jax.numpy as jnp
from jax import lax
from jax.experimental import pallas as pl
from jax.experimental.pallas import tpu as pltpu
from jax.sharding import PartitionSpec as P

EPSILON = 1e-06
LEAD = 9
F32, BF16 = jnp.float32, jnp.bfloat16


def any_sections(sections, experts, tokens, norm_gain, router, w_gate, w_up, w_down, expert_ids):
    tok_count, model_width = tokens.shape
    top_count = expert_ids.shape[1]
    cap = tok_count * top_count * 3 // (2 * experts)
    width = model_width // sections
    half = experts // 2
    chips = experts // 4
    me = lax.axis_index("expert")
    section = lax.axis_index("section")

    def swap(value, mask):
        return lax.ppermute(value, "expert", [(i, i ^ mask) for i in range(experts)])

    tokens_f = tokens.astype(F32)
    mean_sq = jnp.mean(tokens_f * tokens_f, axis=-1, keepdims=True)
    normed = (tokens_f * lax.rsqrt(mean_sq + EPSILON) * norm_gain.astype(F32)).astype(BF16)
    mine = lax.dynamic_slice_in_dim(normed, section * width, width, 1)

    def table(ids):
        named = jnp.any(ids[:, :, None] == jnp.arange(experts, dtype=jnp.int32), axis=1)
        rows = lax.broadcasted_iota(jnp.int32, (tok_count, tok_count), 0)
        cols = lax.broadcasted_iota(jnp.int32, (tok_count, tok_count), 1)
        before = jnp.dot(
            (cols < rows).astype(BF16), named.astype(BF16), preferred_element_type=F32
        )
        return named, jnp.where(named, before, -1.0)

    ids_core = swap(expert_ids, 1)
    ids_far = swap(expert_ids, half)
    ids_far_core = swap(expert_ids, half + 1)
    named, table_own = table(expert_ids)
    logits = jnp.dot(normed, router, preferred_element_type=F32)
    scores = jnp.where(named, jax.nn.sigmoid(logits), 0.0)
    weight = 2.5 * scores / jnp.sum(scores, axis=1, keepdims=True)
    weight_core = swap(weight, 1)
    weight_far = swap(weight, half)
    weight_far_core = swap(weight, half + 1)

    near = (((me // 2) ^ jnp.arange(chips, dtype=jnp.int32)) * 2 + me % 2)[:, None]
    near = (near == jnp.arange(experts, dtype=jnp.int32)[None, :]).astype(F32)

    def columns(first, second):
        both = jnp.concatenate([first, second], axis=0)
        return lax.dot_general(
            near, both, (((1,), (1,)), ((), ())), precision=lax.Precision.HIGHEST,
            preferred_element_type=F32,
        )

    row = lax.broadcasted_iota(jnp.int32, (1, 2 * cap, 2 * tok_count), 1)
    col = lax.broadcasted_iota(jnp.int32, (1, 2 * cap, 2 * tok_count), 2)
    wanted = jnp.where(row // cap == col // tok_count, row % cap, -2).astype(F32)

    def choose(first, second):
        return columns(first, second)[:, None, :] == wanted

    def pick(chosen, toks):
        flat = chosen.astype(BF16).reshape(chips * 2 * cap, 2 * tok_count)
        return jnp.dot(flat, toks, preferred_element_type=F32).astype(BF16).reshape(
            chips, 2 * cap, toks.shape[1]
        )

    def spread(rows):
        return jnp.concatenate(
            [rows[:1]] + [swap(rows[q : q + 1], 2 * q) for q in range(1, chips)], axis=0
        )

    def feature_exchange(rows):
        rows = rows.reshape(chips * 2 * cap, rows.shape[2])
        if sections == 2:
            other = lax.ppermute(rows, "section", [(0, 1), (1, 0)])
            low = jnp.where(section == 0, rows, other)
            high = jnp.where(section == 0, other, rows)
            return jnp.concatenate([low, high], axis=1)
        return lax.all_gather(rows, "section", axis=1, tiled=True)

    def experts_of(full):
        gate_act = jnp.dot(full, w_gate[0], preferred_element_type=F32)
        up_act = jnp.dot(full, w_up[0], preferred_element_type=F32)
        hidden = (jax.nn.silu(gate_act) * up_act).astype(BF16)
        part = jnp.dot(hidden, w_down[0], preferred_element_type=F32).astype(BF16)
        if sections == 2:
            keep = lax.dynamic_slice_in_dim(part, section * width, width, 1)
            give = lax.dynamic_slice_in_dim(part, (1 - section) * width, width, 1)
            got = lax.ppermute(give, "section", [(0, 1), (1, 0)])
            done = (keep.astype(F32) + got.astype(F32)).astype(BF16)
        else:
            done = lax.psum_scatter(part, "section", scatter_dimension=1, tiled=True)
        return done.reshape(chips, 2 * cap, width)

    def mix(chosen, first, second, rows):
        factors = jnp.where(chosen, columns(first, second)[:, None, :], 0.0).astype(BF16)
        factors = factors.reshape(chips * 2 * cap, 2 * tok_count)
        both = lax.dot_general(
            factors, rows.reshape(chips * 2 * cap, width), (((0,), (0,)), ((), ())),
            preferred_element_type=F32,
        )
        got = swap(both[tok_count:].astype(BF16), 1)
        return both[:tok_count] + got.astype(F32)

    chosen_near = choose(table_own, table(ids_core)[1])
    toks_near = jnp.concatenate([mine, swap(mine, 1)], axis=0)
    full_near = feature_exchange(spread(pick(chosen_near, toks_near)))
    far = swap(mine, half)
    chosen_far = choose(table(ids_far)[1], table(ids_far_core)[1])
    toks_far = jnp.concatenate([far, swap(far, 1)], axis=0)
    full_far = feature_exchange(spread(pick(chosen_far, toks_far)))

    back_near = spread(experts_of(full_near))
    back_far = spread(experts_of(full_far))
    sum_far = swap(mix(chosen_far, weight_far, weight_far_core, back_far).astype(BF16), half)
    sum_near = mix(chosen_near, weight, weight_core, back_near)
    residual = lax.dynamic_slice_in_dim(tokens, section * width, width, 1)
    return (residual.astype(F32) + sum_near + sum_far.astype(F32)).astype(BF16)


def prepare_body(experts, place, *refs):
    out, first, second = refs[4:7]
    tokens, gain, router, ids, sems = refs[7:]
    copies = [
        pltpu.make_async_copy(source, target, sems.at[i])
        for i, (source, target) in enumerate(zip(refs[:4], refs[7:11]))
    ]
    for copy in copies:
        copy.start()
    for copy in copies:
        copy.wait()
    tok_count, model_width = tokens.shape
    width = model_width // 2
    tokens_f = tokens[...].astype(F32)
    mean_sq = jnp.mean(tokens_f * tokens_f, axis=-1, keepdims=True)
    gain_f = gain[...].reshape(1, model_width).astype(F32)
    normed = (tokens_f * lax.rsqrt(mean_sq + EPSILON) * gain_f).astype(BF16)
    by_feature = (((1,), (1,)), ((), ()))
    logits = lax.dot_general(router[...], normed, by_feature, preferred_element_type=F32)
    expert = lax.broadcasted_iota(jnp.int32, (experts, tok_count), 0)
    named = ids[0:1, :] == expert
    for k in range(1, ids.shape[0]):
        named = named | (ids[k : k + 1, :] == expert)
    rows = lax.broadcasted_iota(jnp.int32, (tok_count, tok_count), 0)
    cols = lax.broadcasted_iota(jnp.int32, (tok_count, tok_count), 1)
    before = jnp.dot(
        named.astype(F32).astype(BF16),
        (rows < cols).astype(F32).astype(BF16),
        preferred_element_type=F32,
    )
    slot = jnp.where(named, before, -1.0)
    scores = jnp.where(named, 1.0 / (1.0 + jnp.exp(-logits)), 0.0)
    weight = 2.5 * scores / jnp.sum(scores, axis=0, keepdims=True)
    meta = jnp.concatenate(
        [slot, weight, jnp.zeros((128 - 2 * experts, tok_count), F32)], axis=0
    ).astype(BF16)
    meta = lax.dot_general(
        (rows == cols).astype(F32).astype(BF16), meta, by_feature, preferred_element_type=F32
    )
    meta = meta.astype(BF16)
    swapped = place[0] == 1
    low, high = normed[:, :width], normed[:, width:]
    mine = jnp.where(swapped, high, low)
    out[:, :width] = mine
    out[:, width:model_width] = jnp.where(swapped, low, high)
    out[:, model_width:] = meta
    first[:, : width // 2] = mine[:, : width // 2]
    first[:, width // 2 :] = meta
    second[...] = mine[:, width // 2 :]


def prepare(experts, place, tokens, norm_gain, router, expert_ids):
    tok_count, model_width = tokens.shape
    arrays = (tokens, norm_gain, router.T, expert_ids.T)
    return pl.pallas_call(
        functools.partial(prepare_body, experts),
        out_shape=[
            jax.ShapeDtypeStruct((tok_count, columns), BF16)
            for columns in (model_width + 128, model_width // 4 + 128, model_width // 4)
        ],
        in_specs=[pl.BlockSpec(memory_space=pltpu.SMEM)] + [pl.BlockSpec(memory_space=pl.ANY)] * 4,
        out_specs=[pl.BlockSpec(memory_space=pltpu.VMEM)] * 3,
        scratch_shapes=[pltpu.VMEM(a.shape, a.dtype) for a in arrays]
        + [pltpu.SemaphoreType.DMA((4,))],
        compiler_params=pltpu.CompilerParams(vmem_limit_bytes=60 * 1024 * 1024),
        name="prepare",
    )(place, *arrays)


def mlp_body(plan, steps, carried, outs, columns, cap, place, *refs):
    count = 1 + max(piece for _, where in plan for piece, _ in where.values())
    pieces, (w_gate, w_up, w_down) = refs[:count], refs[count : count + 3]
    refs = refs[count + 3 :]
    before = refs[:2] if carried else ()
    refs = refs[2:] if carried else refs
    results, (gate_w, up_w, down_w, in_sems, down_sems) = refs[:-5], refs[-5:]
    model_width, hidden_width = w_gate.shape[1], w_gate.shape[2]
    step = gate_w.shape[1]
    total = model_width // step

    def start_of(first):
        moved = jnp.where(place[0] == first // (model_width // 2), 0, model_width // 2)
        return pl.multiple_of(moved + first % (model_width // 2), 128)

    def load(at, number):
        rows = pl.ds(start_of(number * step), step)
        return (
            pltpu.make_async_copy(w_gate.at[0, rows, :], gate_w.at[at], in_sems.at[0, at]),
            pltpu.make_async_copy(w_up.at[0, rows, :], up_w.at[at], in_sems.at[1, at]),
        )

    def load_down(number):
        first, size = columns[number]
        return pltpu.make_async_copy(
            w_down.at[0, :, pl.ds(start_of(first), size)],
            down_w.at[:, pl.ds(first, size)],
            down_sems.at[number],
        )

    for at, number in enumerate(steps):
        for copy in load(at, number):
            copy.start()
    for number in range(len(columns)):
        load_down(number).start()
    gates, ups = [], []
    first = 0
    for rows, _ in plan:
        for sums, ref in zip((gates, ups), before or (None, None)):
            zero = jnp.zeros((rows, hidden_width), F32)
            sums.append(zero if ref is None else ref[first : first + rows, :])
        first += rows
    for at, number in enumerate(steps):
        for copy in load(at, number):
            copy.wait()
        for b, (_, where) in enumerate(plan):
            piece, column = where[number]
            x = pieces[piece][:, column : column + step]
            gates[b] += jnp.dot(x, gate_w[at], preferred_element_type=F32)
            ups[b] += jnp.dot(x, up_w[at], preferred_element_type=F32)
    if not outs:
        first = 0
        for gate, up in zip(gates, ups):
            for ref, value in zip(results, (gate, up)):
                ref[first : first + value.shape[0], :] = value
            first += gate.shape[0]
        return
    hidden = [(g / (1.0 + jnp.exp(-g)) * u).astype(BF16) for g, u in zip(gates, ups)]
    if cap:
        rows = plan[0][0]
        to = lax.broadcasted_iota(jnp.int32, (rows, rows), 0)
        of = lax.broadcasted_iota(jnp.int32, (rows, rows), 1)
        spot = to % (rows // 2)
        moved = spot // cap * 2 * cap + to // (rows // 2) * cap + spot % cap == of
        hidden = [
            jnp.dot(
                moved.astype(F32).astype(BF16), hidden[0], preferred_element_type=F32
            ).astype(BF16)
        ]
    for number, (left, size) in enumerate(columns):
        load_down(number).wait()
        first = 0
        for h in hidden:
            y = jnp.dot(h, down_w[:, left : left + size], preferred_element_type=F32).astype(BF16)
            for (start, rows, out_left, out_size), ref in zip(outs, results):
                low, high = max(start, first), min(start + rows, first + h.shape[0])
                if out_left <= left < out_left + out_size and low < high:
                    at = left - out_left
                    ref[low - start : high - start, at : at + size] = y[low - first : high - first]
            first += h.shape[0]


def mlp(place, blocks, steps, before, w_gate, w_up, w_down, outs, columns, cap=0):
    _, model_width, hidden_width = w_gate.shape
    total = 4
    step = model_width // total
    plan, pieces = [], []
    for block in blocks:
        where = {}
        for piece, covers in block:
            for at, number in enumerate(covers):
                where[number] = (len(pieces), at * step)
            pieces.append(piece)
        plan.append((block[0][0].shape[0], where))
    rows = sum(r for r, _ in plan)
    vmem = pl.BlockSpec(memory_space=pltpu.VMEM)
    if outs:
        shapes = [jax.ShapeDtypeStruct((r, c), BF16) for _, r, _, c in outs]
    else:
        shapes = [jax.ShapeDtypeStruct((rows, hidden_width), F32)] * 2
    return pl.pallas_call(
        functools.partial(mlp_body, plan, steps, bool(before), outs, columns, cap),
        out_shape=shapes,
        in_specs=[pl.BlockSpec(memory_space=pltpu.SMEM)]
        + [vmem] * len(pieces)
        + [pl.BlockSpec(memory_space=pl.ANY)] * 3
        + [vmem] * len(before),
        out_specs=[vmem] * len(shapes),
        scratch_shapes=[
            pltpu.VMEM((len(steps), step, hidden_width), BF16),
            pltpu.VMEM((len(steps), step, hidden_width), BF16),
            pltpu.VMEM((hidden_width, model_width if outs else 128), BF16),
            pltpu.SemaphoreType.DMA((2, len(steps))),
            pltpu.SemaphoreType.DMA((max(1, len(columns)),)),
        ],
        compiler_params=pltpu.CompilerParams(vmem_limit_bytes=40 * 1024 * 1024),
        cost_estimate=pl.CostEstimate(
            flops=4 * rows * step * len(steps) * hidden_width
            + (2 * rows * model_width * hidden_width if outs else 0),
            bytes_accessed=4 * step * len(steps) * hidden_width
            + (2 * model_width * hidden_width if outs else 0),
            transcendentals=rows * hidden_width if outs else 0,
        ),
        name="mlp",
    )(place, *pieces, w_gate, w_up, w_down, *before)


def join_body(cap, column, keep, crossed, beside, slanted, *outs):
    rows, width = keep.shape
    first = (keep[...].astype(F32) + crossed[...].astype(F32)).astype(BF16)
    second = beside[:, column : column + width].astype(F32) + slanted[...].astype(F32)
    second = second.astype(BF16)
    to = lax.broadcasted_iota(jnp.int32, (2 * cap, rows), 0)
    of = lax.broadcasted_iota(jnp.int32, (2 * cap, rows), 1)
    for q, out in enumerate(outs):
        here = (q * cap + to % cap == of).astype(F32)
        out[...] = (
            jnp.dot(jnp.where(to < cap, here, 0.0).astype(BF16), first, preferred_element_type=F32)
            + jnp.dot(jnp.where(to < cap, 0.0, here).astype(BF16), second, preferred_element_type=F32)
        ).astype(BF16)


def join(cap, chips, column, keep, crossed, beside, slanted):
    vmem = pl.BlockSpec(memory_space=pltpu.VMEM)
    return pl.pallas_call(
        functools.partial(join_body, cap, column),
        out_shape=[jax.ShapeDtypeStruct((2 * cap, keep.shape[1]), BF16)] * chips,
        in_specs=[vmem] * 4,
        out_specs=[vmem] * chips,
        compiler_params=pltpu.CompilerParams(vmem_limit_bytes=32 * 1024 * 1024),
        name="join",
    )(keep, crossed, beside, slanted)


def two_sections(experts, tokens, norm_gain, router, w_gate, w_up, w_down, expert_ids):
    tok_count, model_width = tokens.shape
    top_count = expert_ids.shape[1]
    cap = tok_count * top_count * 3 // (2 * experts)
    width = model_width // 2
    half = experts // 2
    chips = experts // 4
    me = lax.axis_index("expert")
    section = lax.axis_index("section")
    place = jnp.reshape(section, (1,)).astype(jnp.int32)
    group = 2 * cap

    def swap(value, mask):
        return lax.ppermute(value, "expert", [(i, i ^ mask) for i in range(experts)])

    def cross(value):
        return lax.ppermute(value, "section", [(0, 1), (1, 0)])

    packed, mine_0, mine_1 = prepare(experts, place, tokens, norm_gain, router, expert_ids)
    beside = swap(packed, 1)

    near = (((me // 2) ^ jnp.arange(chips, dtype=jnp.int32)) * 2 + me % 2)[:, None]
    lanes = jnp.arange(128, dtype=jnp.int32)[None, :]
    near = jnp.concatenate([near == lanes, near + experts == lanes], axis=0).astype(BF16)
    row = lax.broadcasted_iota(jnp.int32, (1, group, 2 * tok_count), 1)
    col = lax.broadcasted_iota(jnp.int32, (1, group, 2 * tok_count), 2)
    wanted = jnp.where(row // cap == col // tok_count, row % cap, -2).astype(F32)

    def tables(first, second):
        found = jnp.concatenate(
            [
                lax.dot_general(near, m, (((1,), (1,)), ((), ())), preferred_element_type=F32)
                for m in (first, second)
            ],
            axis=1,
        )
        chosen = found[:chips, None, :] == wanted
        factors = jnp.where(chosen, found[chips:, None, :], 0.0).astype(BF16)
        return chosen.astype(BF16), factors.reshape(chips * group, 2 * tok_count)

    def pick(chosen, first, second):
        flat = chosen.reshape(-1, 2 * tok_count)
        return (
            jnp.dot(flat[:, :tok_count], first, preferred_element_type=F32)
            + jnp.dot(flat[:, tok_count:], second, preferred_element_type=F32)
        ).astype(BF16)

    def pieces_of(rows, number):
        return [rows[q * group : (q + 1) * group] for q in range(number)]

    def spread(pieces):
        return [swap(piece, 2 * q) if q else piece for q, piece in enumerate(pieces)]

    def mix(factors, rows):
        return lax.dot_general(
            factors, rows, (((0,), (0,)), ((), ())), preferred_element_type=F32
        )

    def stage(*values):
        return lax.optimization_barrier(values)

    def core_sum(mixed):
        got = swap(mixed[tok_count:].astype(BF16), 1)
        return mixed[:tok_count], got

    weights = (w_gate, w_up, w_down)
    part = width // 2
    meta = packed[:, model_width:]
    far_0 = swap(mine_0, half)

    chosen, factors = tables(meta, beside[:, model_width:])
    some = pieces_of(pick(chosen[2:], packed[:, :width], beside[:, :width]), chips - 2)
    whole = pick(chosen[:2], packed[:, :model_width], beside[:, :model_width])
    far_1 = swap(stage(mine_1, some)[0], half)
    some = [swap(piece, 2 * q) for q, piece in enumerate(some, 2)]
    whole_near = swap(whole[group:], 2)
    some, whole_0, whole_near, far_0, far_1 = stage(some, whole[:group], whole_near, far_0, far_1)

    some = jnp.concatenate(some, axis=0)
    some_other = cross(some)
    beside_0 = swap(far_0, 1)
    far_chosen, far_factors = tables(far_0[:, part:], beside_0[:, part:])
    rows_0 = spread(pieces_of(pick(far_chosen, far_0[:, :part], beside_0[:, :part]), chips))
    some, rows_0 = stage(some, rows_0)

    rows_0 = jnp.concatenate(rows_0, axis=0)
    other_0 = cross(rows_0)
    rows_1 = spread(pieces_of(pick(far_chosen, far_1, swap(far_1, 1)), chips))
    whole = jnp.concatenate([whole_0, whole_near], axis=0)
    all_rows = chips * group
    (near,) = mlp(
        place, [[(whole, (0, 1, 2, 3))], [(some, (0, 1)), (some_other, (2, 3))]],
        (0, 1, 2, 3), (), *weights, [(0, all_rows, 0, model_width)],
        [(k * part, part) for k in range(4)],
    )
    rows_0, rows_1, near = stage(rows_0, rows_1, near)

    rows_1 = jnp.concatenate(rows_1, axis=0)
    other_1 = cross(rows_1)
    near = pieces_of(near, chips)
    near_back = near[:1] + [swap(near[q], 2 * q) for q in range(1, chips - 1)]
    near_last = swap(near[-1], 2 * (chips - 1))
    sums = mlp(
        place, [[(rows_0, (0,)), (rows_1, (1,)), (other_0, (2,))]], (0, 1, 2), (), *weights, (), ()
    )
    other_1, near_back, sums = stage(other_1, near_back, sums)

    lead = min(width - 128, (LEAD * width // 14 + 127) // 128 * 128)
    columns = [(width, lead), (width + lead, width - lead), (0, lead), (lead, width - lead)]
    outs = mlp(
        place, [[(other_1, (3,))]], (3,), sums, *weights, [(0, all_rows, *c) for c in columns], columns
    )
    (give_0, give_1, keep_0, keep_1), near_back = stage(outs, near_back)
    got_0 = cross(give_0)
    got_1 = cross(give_1)
    got_0, near_last, near_back = stage(got_0, near_last, near_back)

    back_0 = spread(pieces_of((keep_0.astype(F32) + got_0.astype(F32)).astype(BF16), chips))
    near_sum = mix(factors, jnp.concatenate(near_back + [near_last], axis=0))
    far_0, far_0_core = core_sum(mix(far_factors, jnp.concatenate(back_0, axis=0)))
    got_1, far_0, far_0_core, near_sum = stage(got_1, far_0, far_0_core, near_sum)

    far_0 = swap((far_0 + far_0_core.astype(F32)).astype(BF16), half)
    back_1 = spread(pieces_of((keep_1.astype(F32) + got_1.astype(F32)).astype(BF16), chips))
    near_sum, near_core = core_sum(near_sum)
    far_1, far_1_core = core_sum(mix(far_factors, jnp.concatenate(back_1, axis=0)))
    near_sum, near_core, far_0, far_1, far_1_core = stage(near_sum, near_core, far_0, far_1, far_1_core)

    far_1 = (far_1 + far_1_core.astype(F32)).astype(BF16)
    far_1 = swap(far_1, half)
    near_sum = near_sum + near_core.astype(F32)
    near_got = cross(near_sum[:, width:].astype(BF16))
    residual = lax.dynamic_slice_in_dim(tokens, section * width, width, 1)
    near_sum = residual.astype(F32) + near_sum[:, :width] + near_got.astype(F32)
    first = (near_sum[:, :lead] + far_0.astype(F32)).astype(BF16)
    first, rest = stage(first, near_sum[:, lead:])
    return jnp.concatenate([first, (rest + far_1.astype(F32)).astype(BF16)], axis=1)


def solution(mesh):
    placed = (
        P("expert", None),
        P(),
        P(),
        P("expert", None, "section"),
        P("expert", None, "section"),
        P("expert", "section", None),
        P("expert", None),
    )

    def body(*args):
        sections, experts = mesh.shape["section"], mesh.shape["expert"]
        if sections == 2 and experts <= 64:
            return two_sections(experts, *args)
        return any_sections(sections, experts, *args)

    return jax.shard_map(
        body, mesh=mesh, in_specs=placed, out_specs=P("expert", "section"), check_vma=False
    )
```

```python
import functools

import jax
import jax.numpy as jnp
from jax import lax
from jax.experimental import pallas as pl
from jax.experimental.pallas import tpu as pltpu
from jax.sharding import PartitionSpec as P

EPSILON = 1e-06
LEAD = 9
F32, BF16 = jnp.float32, jnp.bfloat16


def any_sections(sections, experts, tokens, norm_gain, router, w_gate, w_up, w_down, expert_ids):
    tok_count, model_width = tokens.shape
    top_count = expert_ids.shape[1]
    cap = tok_count * top_count * 3 // (2 * experts)
    width = model_width // sections
    half = experts // 2
    chips = experts // 4
    me = lax.axis_index("expert")
    section = lax.axis_index("section")

    def swap(value, mask):
        return lax.ppermute(value, "expert", [(i, i ^ mask) for i in range(experts)])

    tokens_f = tokens.astype(F32)
    mean_sq = jnp.mean(tokens_f * tokens_f, axis=-1, keepdims=True)
    normed = (tokens_f * lax.rsqrt(mean_sq + EPSILON) * norm_gain.astype(F32)).astype(BF16)
    mine = lax.dynamic_slice_in_dim(normed, section * width, width, 1)

    def table(ids):
        named = jnp.any(ids[:, :, None] == jnp.arange(experts, dtype=jnp.int32), axis=1)
        rows = lax.broadcasted_iota(jnp.int32, (tok_count, tok_count), 0)
        cols = lax.broadcasted_iota(jnp.int32, (tok_count, tok_count), 1)
        before = jnp.dot(
            (cols < rows).astype(BF16), named.astype(BF16), preferred_element_type=F32
        )
        return named, jnp.where(named, before, -1.0)

    ids_core = swap(expert_ids, 1)
    ids_far = swap(expert_ids, half)
    ids_far_core = swap(expert_ids, half + 1)
    named, table_own = table(expert_ids)
    logits = jnp.dot(normed, router, preferred_element_type=F32)
    scores = jnp.where(named, jax.nn.sigmoid(logits), 0.0)
    weight = 2.5 * scores / jnp.sum(scores, axis=1, keepdims=True)
    weight_core = swap(weight, 1)
    weight_far = swap(weight, half)
    weight_far_core = swap(weight, half + 1)

    near = (((me // 2) ^ jnp.arange(chips, dtype=jnp.int32)) * 2 + me % 2)[:, None]
    near = (near == jnp.arange(experts, dtype=jnp.int32)[None, :]).astype(F32)

    def columns(first, second):
        both = jnp.concatenate([first, second], axis=0)
        return lax.dot_general(
            near, both, (((1,), (1,)), ((), ())), precision=lax.Precision.HIGHEST,
            preferred_element_type=F32,
        )

    row = lax.broadcasted_iota(jnp.int32, (1, 2 * cap, 2 * tok_count), 1)
    col = lax.broadcasted_iota(jnp.int32, (1, 2 * cap, 2 * tok_count), 2)
    wanted = jnp.where(row // cap == col // tok_count, row % cap, -2).astype(F32)

    def choose(first, second):
        return columns(first, second)[:, None, :] == wanted

    def pick(chosen, toks):
        flat = chosen.astype(BF16).reshape(chips * 2 * cap, 2 * tok_count)
        return jnp.dot(flat, toks, preferred_element_type=F32).astype(BF16).reshape(
            chips, 2 * cap, toks.shape[1]
        )

    def spread(rows):
        return jnp.concatenate(
            [rows[:1]] + [swap(rows[q : q + 1], 2 * q) for q in range(1, chips)], axis=0
        )

    def feature_exchange(rows):
        rows = rows.reshape(chips * 2 * cap, rows.shape[2])
        if sections == 2:
            other = lax.ppermute(rows, "section", [(0, 1), (1, 0)])
            low = jnp.where(section == 0, rows, other)
            high = jnp.where(section == 0, other, rows)
            return jnp.concatenate([low, high], axis=1)
        return lax.all_gather(rows, "section", axis=1, tiled=True)

    def experts_of(full):
        gate_act = jnp.dot(full, w_gate[0], preferred_element_type=F32)
        up_act = jnp.dot(full, w_up[0], preferred_element_type=F32)
        hidden = (jax.nn.silu(gate_act) * up_act).astype(BF16)
        part = jnp.dot(hidden, w_down[0], preferred_element_type=F32).astype(BF16)
        if sections == 2:
            keep = lax.dynamic_slice_in_dim(part, section * width, width, 1)
            give = lax.dynamic_slice_in_dim(part, (1 - section) * width, width, 1)
            got = lax.ppermute(give, "section", [(0, 1), (1, 0)])
            done = (keep.astype(F32) + got.astype(F32)).astype(BF16)
        else:
            done = lax.psum_scatter(part, "section", scatter_dimension=1, tiled=True)
        return done.reshape(chips, 2 * cap, width)

    def mix(chosen, first, second, rows):
        factors = jnp.where(chosen, columns(first, second)[:, None, :], 0.0).astype(BF16)
        factors = factors.reshape(chips * 2 * cap, 2 * tok_count)
        both = lax.dot_general(
            factors, rows.reshape(chips * 2 * cap, width), (((0,), (0,)), ((), ())),
            preferred_element_type=F32,
        )
        got = swap(both[tok_count:].astype(BF16), 1)
        return both[:tok_count] + got.astype(F32)

    chosen_near = choose(table_own, table(ids_core)[1])
    toks_near = jnp.concatenate([mine, swap(mine, 1)], axis=0)
    full_near = feature_exchange(spread(pick(chosen_near, toks_near)))
    far = swap(mine, half)
    chosen_far = choose(table(ids_far)[1], table(ids_far_core)[1])
    toks_far = jnp.concatenate([far, swap(far, 1)], axis=0)
    full_far = feature_exchange(spread(pick(chosen_far, toks_far)))

    back_near = spread(experts_of(full_near))
    back_far = spread(experts_of(full_far))
    sum_far = swap(mix(chosen_far, weight_far, weight_far_core, back_far).astype(BF16), half)
    sum_near = mix(chosen_near, weight, weight_core, back_near)
    residual = lax.dynamic_slice_in_dim(tokens, section * width, width, 1)
    return (residual.astype(F32) + sum_near + sum_far.astype(F32)).astype(BF16)


def prepare_body(experts, place, *refs):
    out, first, second = refs[4:7]
    tokens, gain, router, ids, sems = refs[7:]
    copies = [
        pltpu.make_async_copy(source, target, sems.at[i])
        for i, (source, target) in enumerate(zip(refs[:4], refs[7:11]))
    ]
    for copy in copies:
        copy.start()
    for copy in copies:
        copy.wait()
    tok_count, model_width = tokens.shape
    width = model_width // 2
    tokens_f = tokens[...].astype(F32)
    mean_sq = jnp.mean(tokens_f * tokens_f, axis=-1, keepdims=True)
    gain_f = gain[...].reshape(1, model_width).astype(F32)
    normed = (tokens_f * lax.rsqrt(mean_sq + EPSILON) * gain_f).astype(BF16)
    by_feature = (((1,), (1,)), ((), ()))
    logits = lax.dot_general(router[...], normed, by_feature, preferred_element_type=F32)
    expert = lax.broadcasted_iota(jnp.int32, (experts, tok_count), 0)
    named = ids[0:1, :] == expert
    for k in range(1, ids.shape[0]):
        named = named | (ids[k : k + 1, :] == expert)
    rows = lax.broadcasted_iota(jnp.int32, (tok_count, tok_count), 0)
    cols = lax.broadcasted_iota(jnp.int32, (tok_count, tok_count), 1)
    before = jnp.dot(
        named.astype(F32).astype(BF16),
        (rows < cols).astype(F32).astype(BF16),
        preferred_element_type=F32,
    )
    slot = jnp.where(named, before, -1.0)
    scores = jnp.where(named, 1.0 / (1.0 + jnp.exp(-logits)), 0.0)
    weight = 2.5 * scores / jnp.sum(scores, axis=0, keepdims=True)
    meta = jnp.concatenate(
        [slot, weight, jnp.zeros((128 - 2 * experts, tok_count), F32)], axis=0
    ).astype(BF16)
    meta = lax.dot_general(
        (rows == cols).astype(F32).astype(BF16), meta, by_feature, preferred_element_type=F32
    )
    meta = meta.astype(BF16)
    swapped = place[0] == 1
    low, high = normed[:, :width], normed[:, width:]
    mine = jnp.where(swapped, high, low)
    out[:, :width] = mine
    out[:, width:model_width] = jnp.where(swapped, low, high)
    out[:, model_width:] = meta
    first[:, : width // 2] = mine[:, : width // 2]
    first[:, width // 2 :] = meta
    second[...] = mine[:, width // 2 :]


def prepare(experts, place, tokens, norm_gain, router, expert_ids):
    tok_count, model_width = tokens.shape
    arrays = (tokens, norm_gain, router.T, expert_ids.T)
    return pl.pallas_call(
        functools.partial(prepare_body, experts),
        out_shape=[
            jax.ShapeDtypeStruct((tok_count, columns), BF16)
            for columns in (model_width + 128, model_width // 4 + 128, model_width // 4)
        ],
        in_specs=[pl.BlockSpec(memory_space=pltpu.SMEM)] + [pl.BlockSpec(memory_space=pl.ANY)] * 4,
        out_specs=[pl.BlockSpec(memory_space=pltpu.VMEM)] * 3,
        scratch_shapes=[pltpu.VMEM(a.shape, a.dtype) for a in arrays]
        + [pltpu.SemaphoreType.DMA((4,))],
        compiler_params=pltpu.CompilerParams(vmem_limit_bytes=60 * 1024 * 1024),
        name="prepare",
    )(place, *arrays)


def mlp_body(plan, steps, carried, outs, columns, hand, place, *refs):
    count = 1 + max(piece for _, where in plan for piece, _ in where.values())
    pieces, (w_gate, w_up, w_down) = refs[:count], refs[count : count + 3]
    refs = refs[count + 3 :]
    before = refs[:2] if carried else ()
    refs = refs[2:] if carried else refs
    results, (gate_w, up_w, down_w, in_sems, down_sems) = refs[:-5], refs[-5:]
    model_width, hidden_width = w_gate.shape[1], w_gate.shape[2]
    step = gate_w.shape[1]
    total = model_width // step

    def start_of(first):
        moved = jnp.where(place[0] == first // (model_width // 2), 0, model_width // 2)
        return pl.multiple_of(moved + first % (model_width // 2), 128)

    def load(at, number):
        rows = pl.ds(start_of(number * step), step)
        return (
            pltpu.make_async_copy(w_gate.at[0, rows, :], gate_w.at[at], in_sems.at[0, at]),
            pltpu.make_async_copy(w_up.at[0, rows, :], up_w.at[at], in_sems.at[1, at]),
        )

    def load_down(number):
        first, size = columns[number]
        return pltpu.make_async_copy(
            w_down.at[0, :, pl.ds(start_of(first), size)],
            down_w.at[:, pl.ds(first, size)],
            down_sems.at[number],
        )

    for at, number in enumerate(steps):
        for copy in load(at, number):
            copy.start()
    for number in range(len(columns)):
        load_down(number).start()
    gates, ups = [], []
    first = 0
    for rows, _ in plan:
        for sums, ref in zip((gates, ups), before or (None, None)):
            zero = jnp.zeros((rows, hidden_width), F32)
            sums.append(zero if ref is None else ref[first : first + rows, :])
        first += rows
    for at, number in enumerate(steps):
        for copy in load(at, number):
            copy.wait()
        for b, (_, where) in enumerate(plan):
            piece, column = where[number]
            x = pieces[piece][:, column : column + step]
            gates[b] += jnp.dot(x, gate_w[at], preferred_element_type=F32)
            ups[b] += jnp.dot(x, up_w[at], preferred_element_type=F32)
    if not outs:
        first = 0
        for gate, up in zip(gates, ups):
            for ref, value in zip(results, (gate, up)):
                ref[first : first + value.shape[0], :] = value
            first += gate.shape[0]
        return
    hidden = [(g / (1.0 + jnp.exp(-g)) * u).astype(BF16) for g, u in zip(gates, ups)]
    if hand:
        results[-1][...] = hidden[0]
    for number, (left, size) in enumerate(columns):
        load_down(number).wait()
        first = 0
        for h in hidden:
            y = jnp.dot(h, down_w[:, left : left + size], preferred_element_type=F32).astype(BF16)
            for (start, rows, out_left, out_size), ref in zip(outs, results):
                low, high = max(start, first), min(start + rows, first + h.shape[0])
                if out_left <= left < out_left + out_size and low < high:
                    at = left - out_left
                    ref[low - start : high - start, at : at + size] = y[low - first : high - first]
            first += h.shape[0]


def mlp(place, blocks, steps, before, w_gate, w_up, w_down, outs, columns, hand=False):
    _, model_width, hidden_width = w_gate.shape
    total = 4
    step = model_width // total
    plan, pieces = [], []
    for block in blocks:
        where = {}
        for piece, covers in block:
            for at, number in enumerate(covers):
                where[number] = (len(pieces), at * step)
            pieces.append(piece)
        plan.append((block[0][0].shape[0], where))
    rows = sum(r for r, _ in plan)
    vmem = pl.BlockSpec(memory_space=pltpu.VMEM)
    if outs:
        shapes = [jax.ShapeDtypeStruct((r, c), BF16) for _, r, _, c in outs]
        shapes += [jax.ShapeDtypeStruct((rows, hidden_width), BF16)] * hand
    else:
        shapes = [jax.ShapeDtypeStruct((rows, hidden_width), F32)] * 2
    return pl.pallas_call(
        functools.partial(mlp_body, plan, steps, bool(before), outs, columns, hand),
        out_shape=shapes,
        in_specs=[pl.BlockSpec(memory_space=pltpu.SMEM)]
        + [vmem] * len(pieces)
        + [pl.BlockSpec(memory_space=pl.ANY)] * 3
        + [vmem] * len(before),
        out_specs=[vmem] * len(shapes),
        scratch_shapes=[
            pltpu.VMEM((len(steps), step, hidden_width), BF16),
            pltpu.VMEM((len(steps), step, hidden_width), BF16),
            pltpu.VMEM((hidden_width, model_width if outs else 128), BF16),
            pltpu.SemaphoreType.DMA((2, len(steps))),
            pltpu.SemaphoreType.DMA((max(1, len(columns)),)),
        ],
        compiler_params=pltpu.CompilerParams(vmem_limit_bytes=40 * 1024 * 1024),
        cost_estimate=pl.CostEstimate(
            flops=4 * rows * step * len(steps) * hidden_width
            + (2 * rows * model_width * hidden_width if outs else 0),
            bytes_accessed=4 * step * len(steps) * hidden_width
            + (2 * model_width * hidden_width if outs else 0),
            transcendentals=rows * hidden_width if outs else 0,
        ),
        name="mlp",
    )(place, *pieces, w_gate, w_up, w_down, *before)


def down_body(columns, place, hidden, w_down, *refs):
    outs, (weights, sems) = refs[: len(columns)], refs[len(columns) :]
    width = w_down.shape[2] // 2
    copies = []
    for number, (first, size) in enumerate(columns):
        moved = jnp.where(place[0] == first // width, 0, width) + first % width
        copies.append(pltpu.make_async_copy(
            w_down.at[0, :, pl.ds(pl.multiple_of(moved, 128), size)],
            weights.at[:, pl.ds(first, size)],
            sems.at[number],
        ))
    for copy in copies:
        copy.start()
    for copy, (first, size), out in zip(copies, columns, outs):
        copy.wait()
        out[...] = jnp.dot(
            hidden[...], weights[:, first : first + size], preferred_element_type=F32
        ).astype(BF16)


def down(place, hidden, w_down, columns):
    rows, hidden_width = hidden.shape
    vmem = pl.BlockSpec(memory_space=pltpu.VMEM)
    count = sum(size for _, size in columns)
    return pl.pallas_call(
        functools.partial(down_body, columns),
        out_shape=[jax.ShapeDtypeStruct((rows, size), BF16) for _, size in columns],
        in_specs=[pl.BlockSpec(memory_space=pltpu.SMEM), vmem, pl.BlockSpec(memory_space=pl.ANY)],
        out_specs=[vmem] * len(columns),
        scratch_shapes=[
            pltpu.VMEM((hidden_width, w_down.shape[2]), BF16),
            pltpu.SemaphoreType.DMA((len(columns),)),
        ],
        compiler_params=pltpu.CompilerParams(vmem_limit_bytes=40 * 1024 * 1024),
        cost_estimate=pl.CostEstimate(
            flops=2 * rows * count * hidden_width,
            bytes_accessed=2 * count * hidden_width,
            transcendentals=0,
        ),
        name="down",
    )(place, hidden, w_down)


def two_sections(experts, tokens, norm_gain, router, w_gate, w_up, w_down, expert_ids):
    tok_count, model_width = tokens.shape
    top_count = expert_ids.shape[1]
    cap = tok_count * top_count * 3 // (2 * experts)
    width = model_width // 2
    half = experts // 2
    chips = experts // 4
    me = lax.axis_index("expert")
    section = lax.axis_index("section")
    place = jnp.reshape(section, (1,)).astype(jnp.int32)
    group = 2 * cap

    def swap(value, mask):
        return lax.ppermute(value, "expert", [(i, i ^ mask) for i in range(experts)])

    def cross(value):
        return lax.ppermute(value, "section", [(0, 1), (1, 0)])

    packed, mine_0, mine_1 = prepare(experts, place, tokens, norm_gain, router, expert_ids)
    beside = swap(packed, 1)

    near = (((me // 2) ^ jnp.arange(chips, dtype=jnp.int32)) * 2 + me % 2)[:, None]
    lanes = jnp.arange(128, dtype=jnp.int32)[None, :]
    near = jnp.concatenate([near == lanes, near + experts == lanes], axis=0).astype(BF16)
    row = lax.broadcasted_iota(jnp.int32, (1, group, 2 * tok_count), 1)
    col = lax.broadcasted_iota(jnp.int32, (1, group, 2 * tok_count), 2)
    wanted = jnp.where(row // cap == col // tok_count, row % cap, -2).astype(F32)

    def tables(first, second):
        found = jnp.concatenate(
            [
                lax.dot_general(near, m, (((1,), (1,)), ((), ())), preferred_element_type=F32)
                for m in (first, second)
            ],
            axis=1,
        )
        chosen = found[:chips, None, :] == wanted
        factors = jnp.where(chosen, found[chips:, None, :], 0.0).astype(BF16)
        return chosen.astype(BF16), factors.reshape(chips * group, 2 * tok_count)

    def pick(chosen, first, second):
        flat = chosen.reshape(-1, 2 * tok_count)
        return (
            jnp.dot(flat[:, :tok_count], first, preferred_element_type=F32)
            + jnp.dot(flat[:, tok_count:], second, preferred_element_type=F32)
        ).astype(BF16)

    def pieces_of(rows, number):
        return [rows[q * group : (q + 1) * group] for q in range(number)]

    def spread(pieces):
        return [swap(piece, 2 * q) if q else piece for q, piece in enumerate(pieces)]

    def mix(factors, rows):
        return lax.dot_general(
            factors, rows, (((0,), (0,)), ((), ())), preferred_element_type=F32
        )

    def stage(*values):
        return lax.optimization_barrier(values)

    def core_sum(mixed):
        got = swap(mixed[tok_count:].astype(BF16), 1)
        return mixed[:tok_count], got

    weights = (w_gate, w_up, w_down)
    part = width // 2
    meta = packed[:, model_width:]
    far_0 = swap(mine_0, half)

    chosen, factors = tables(meta, beside[:, model_width:])
    some = pieces_of(pick(chosen[2:], packed[:, :width], beside[:, :width]), chips - 2)
    whole = pick(chosen[:2], packed[:, :model_width], beside[:, :model_width])
    far_1 = swap(stage(mine_1, some)[0], half)
    some = [swap(piece, 2 * q) for q, piece in enumerate(some, 2)]
    whole_near = swap(whole[group:], 2)
    some, whole_0, whole_near, far_0, far_1 = stage(some, whole[:group], whole_near, far_0, far_1)

    some = jnp.concatenate(some, axis=0)
    some_other = cross(some)
    beside_0 = swap(far_0, 1)
    far_chosen, far_factors = tables(far_0[:, part:], beside_0[:, part:])
    rows_0 = spread(pieces_of(pick(far_chosen, far_0[:, :part], beside_0[:, :part]), chips))
    some, rows_0 = stage(some, rows_0)

    rows_0 = jnp.concatenate(rows_0, axis=0)
    other_0 = cross(rows_0)
    rows_1 = spread(pieces_of(pick(far_chosen, far_1, swap(far_1, 1)), chips))
    whole = jnp.concatenate([whole_0, whole_near], axis=0)
    all_rows = chips * group
    (near,) = mlp(
        place, [[(whole, (0, 1, 2, 3))], [(some, (0, 1)), (some_other, (2, 3))]],
        (0, 1, 2, 3), (), *weights, [(0, all_rows, 0, model_width)],
        [(k * part, part) for k in range(4)],
    )
    rows_0, rows_1, near = stage(rows_0, rows_1, near)

    rows_1 = jnp.concatenate(rows_1, axis=0)
    other_1 = cross(rows_1)
    near = pieces_of(near, chips)
    near_back = near[:1] + [swap(near[q], 2 * q) for q in range(1, chips - 1)]
    near_last = swap(near[-1], 2 * (chips - 1))
    sums = mlp(
        place, [[(rows_0, (0,)), (rows_1, (1,)), (other_0, (2,))]], (0, 1, 2), (), *weights, (), ()
    )
    other_1, near_back, sums = stage(other_1, near_back, sums)

    lead = min(width - 128, (LEAD * width // 14 + 127) // 128 * 128)
    columns = [(width + lead, width - lead), (0, lead), (lead, width - lead)]
    give_0, hidden = mlp(
        place, [[(other_1, (3,))]], (3,), sums, *weights,
        [(0, all_rows, width, lead)], [(width, lead)], True,
    )
    give_0, hidden, near_back = stage(give_0, hidden, near_back)
    got_0 = cross(give_0)
    give_1, keep_0, keep_1 = down(place, hidden, w_down, columns)
    got_0, near_last, near_back, give_1 = stage(got_0, near_last, near_back, give_1)
    got_1 = cross(give_1)

    back_0 = spread(pieces_of((keep_0.astype(F32) + got_0.astype(F32)).astype(BF16), chips))
    near_sum = mix(factors, jnp.concatenate(near_back + [near_last], axis=0))
    far_0, far_0_core = core_sum(mix(far_factors, jnp.concatenate(back_0, axis=0)))
    got_1, far_0, far_0_core, near_sum = stage(got_1, far_0, far_0_core, near_sum)

    far_0 = swap((far_0 + far_0_core.astype(F32)).astype(BF16), half)
    back_1 = spread(pieces_of((keep_1.astype(F32) + got_1.astype(F32)).astype(BF16), chips))
    near_sum, near_core = core_sum(near_sum)
    far_1, far_1_core = core_sum(mix(far_factors, jnp.concatenate(back_1, axis=0)))
    near_sum, near_core, far_0, far_1, far_1_core = stage(near_sum, near_core, far_0, far_1, far_1_core)

    far_1 = (far_1 + far_1_core.astype(F32)).astype(BF16)
    far_1 = swap(far_1, half)
    near_sum = near_sum + near_core.astype(F32)
    near_got = cross(near_sum[:, width:].astype(BF16))
    residual = lax.dynamic_slice_in_dim(tokens, section * width, width, 1)
    near_sum = residual.astype(F32) + near_sum[:, :width] + near_got.astype(F32)
    first = (near_sum[:, :lead] + far_0.astype(F32)).astype(BF16)
    first, rest = stage(first, near_sum[:, lead:])
    return jnp.concatenate([first, (rest + far_1.astype(F32)).astype(BF16)], axis=1)


def solution(mesh):
    placed = (
        P("expert", None),
        P(),
        P(),
        P("expert", None, "section"),
        P("expert", None, "section"),
        P("expert", "section", None),
        P("expert", None),
    )

    def body(*args):
        sections, experts = mesh.shape["section"], mesh.shape["expert"]
        if sections == 2 and experts <= 64:
            return two_sections(experts, *args)
        return any_sections(sections, experts, *args)

    return jax.shard_map(
        body, mesh=mesh, in_specs=placed, out_specs=P("expert", "section"), check_vma=False
    )
```

```python
import functools

import jax
import jax.numpy as jnp
from jax import lax
from jax.experimental import pallas as pl
from jax.experimental.pallas import tpu as pltpu
from jax.sharding import PartitionSpec as P

EPSILON = 1e-06
LEAD = 8
F32, BF16 = jnp.float32, jnp.bfloat16


def any_sections(sections, experts, tokens, norm_gain, router, w_gate, w_up, w_down, expert_ids):
    tok_count, model_width = tokens.shape
    top_count = expert_ids.shape[1]
    cap = tok_count * top_count * 3 // (2 * experts)
    width = model_width // sections
    half = experts // 2
    chips = experts // 4
    me = lax.axis_index("expert")
    section = lax.axis_index("section")

    def swap(value, mask):
        return lax.ppermute(value, "expert", [(i, i ^ mask) for i in range(experts)])

    tokens_f = tokens.astype(F32)
    mean_sq = jnp.mean(tokens_f * tokens_f, axis=-1, keepdims=True)
    normed = (tokens_f * lax.rsqrt(mean_sq + EPSILON) * norm_gain.astype(F32)).astype(BF16)
    mine = lax.dynamic_slice_in_dim(normed, section * width, width, 1)

    def table(ids):
        named = jnp.any(ids[:, :, None] == jnp.arange(experts, dtype=jnp.int32), axis=1)
        rows = lax.broadcasted_iota(jnp.int32, (tok_count, tok_count), 0)
        cols = lax.broadcasted_iota(jnp.int32, (tok_count, tok_count), 1)
        before = jnp.dot(
            (cols < rows).astype(BF16), named.astype(BF16), preferred_element_type=F32
        )
        return named, jnp.where(named, before, -1.0)

    ids_core = swap(expert_ids, 1)
    ids_far = swap(expert_ids, half)
    ids_far_core = swap(expert_ids, half + 1)
    named, table_own = table(expert_ids)
    logits = jnp.dot(normed, router, preferred_element_type=F32)
    scores = jnp.where(named, jax.nn.sigmoid(logits), 0.0)
    weight = 2.5 * scores / jnp.sum(scores, axis=1, keepdims=True)
    weight_core = swap(weight, 1)
    weight_far = swap(weight, half)
    weight_far_core = swap(weight, half + 1)

    near = (((me // 2) ^ jnp.arange(chips, dtype=jnp.int32)) * 2 + me % 2)[:, None]
    near = (near == jnp.arange(experts, dtype=jnp.int32)[None, :]).astype(F32)

    def columns(first, second):
        both = jnp.concatenate([first, second], axis=0)
        return lax.dot_general(
            near, both, (((1,), (1,)), ((), ())), precision=lax.Precision.HIGHEST,
            preferred_element_type=F32,
        )

    row = lax.broadcasted_iota(jnp.int32, (1, 2 * cap, 2 * tok_count), 1)
    col = lax.broadcasted_iota(jnp.int32, (1, 2 * cap, 2 * tok_count), 2)
    wanted = jnp.where(row // cap == col // tok_count, row % cap, -2).astype(F32)

    def choose(first, second):
        return columns(first, second)[:, None, :] == wanted

    def pick(chosen, toks):
        flat = chosen.astype(BF16).reshape(chips * 2 * cap, 2 * tok_count)
        return jnp.dot(flat, toks, preferred_element_type=F32).astype(BF16).reshape(
            chips, 2 * cap, toks.shape[1]
        )

    def spread(rows):
        return jnp.concatenate(
            [rows[:1]] + [swap(rows[q : q + 1], 2 * q) for q in range(1, chips)], axis=0
        )

    def feature_exchange(rows):
        rows = rows.reshape(chips * 2 * cap, rows.shape[2])
        if sections == 2:
            other = lax.ppermute(rows, "section", [(0, 1), (1, 0)])
            low = jnp.where(section == 0, rows, other)
            high = jnp.where(section == 0, other, rows)
            return jnp.concatenate([low, high], axis=1)
        return lax.all_gather(rows, "section", axis=1, tiled=True)

    def experts_of(full):
        gate_act = jnp.dot(full, w_gate[0], preferred_element_type=F32)
        up_act = jnp.dot(full, w_up[0], preferred_element_type=F32)
        hidden = (jax.nn.silu(gate_act) * up_act).astype(BF16)
        part = jnp.dot(hidden, w_down[0], preferred_element_type=F32).astype(BF16)
        if sections == 2:
            keep = lax.dynamic_slice_in_dim(part, section * width, width, 1)
            give = lax.dynamic_slice_in_dim(part, (1 - section) * width, width, 1)
            got = lax.ppermute(give, "section", [(0, 1), (1, 0)])
            done = (keep.astype(F32) + got.astype(F32)).astype(BF16)
        else:
            done = lax.psum_scatter(part, "section", scatter_dimension=1, tiled=True)
        return done.reshape(chips, 2 * cap, width)

    def mix(chosen, first, second, rows):
        factors = jnp.where(chosen, columns(first, second)[:, None, :], 0.0).astype(BF16)
        factors = factors.reshape(chips * 2 * cap, 2 * tok_count)
        both = lax.dot_general(
            factors, rows.reshape(chips * 2 * cap, width), (((0,), (0,)), ((), ())),
            preferred_element_type=F32,
        )
        got = swap(both[tok_count:].astype(BF16), 1)
        return both[:tok_count] + got.astype(F32)

    chosen_near = choose(table_own, table(ids_core)[1])
    toks_near = jnp.concatenate([mine, swap(mine, 1)], axis=0)
    full_near = feature_exchange(spread(pick(chosen_near, toks_near)))
    far = swap(mine, half)
    chosen_far = choose(table(ids_far)[1], table(ids_far_core)[1])
    toks_far = jnp.concatenate([far, swap(far, 1)], axis=0)
    full_far = feature_exchange(spread(pick(chosen_far, toks_far)))

    back_near = spread(experts_of(full_near))
    back_far = spread(experts_of(full_far))
    sum_far = swap(mix(chosen_far, weight_far, weight_far_core, back_far).astype(BF16), half)
    sum_near = mix(chosen_near, weight, weight_core, back_near)
    residual = lax.dynamic_slice_in_dim(tokens, section * width, width, 1)
    return (residual.astype(F32) + sum_near + sum_far.astype(F32)).astype(BF16)


def prepare_body(experts, place, *refs):
    out, first, second = refs[4:7]
    tokens, gain, router, ids, sems = refs[7:]
    copies = [
        pltpu.make_async_copy(source, target, sems.at[i])
        for i, (source, target) in enumerate(zip(refs[:4], refs[7:11]))
    ]
    for copy in copies:
        copy.start()
    for copy in copies:
        copy.wait()
    tok_count, model_width = tokens.shape
    width = model_width // 2
    tokens_f = tokens[...].astype(F32)
    mean_sq = jnp.mean(tokens_f * tokens_f, axis=-1, keepdims=True)
    gain_f = gain[...].reshape(1, model_width).astype(F32)
    normed = (tokens_f * lax.rsqrt(mean_sq + EPSILON) * gain_f).astype(BF16)
    by_feature = (((1,), (1,)), ((), ()))
    logits = lax.dot_general(router[...], normed, by_feature, preferred_element_type=F32)
    expert = lax.broadcasted_iota(jnp.int32, (experts, tok_count), 0)
    named = ids[0:1, :] == expert
    for k in range(1, ids.shape[0]):
        named = named | (ids[k : k + 1, :] == expert)
    rows = lax.broadcasted_iota(jnp.int32, (tok_count, tok_count), 0)
    cols = lax.broadcasted_iota(jnp.int32, (tok_count, tok_count), 1)
    before = jnp.dot(
        named.astype(F32).astype(BF16),
        (rows < cols).astype(F32).astype(BF16),
        preferred_element_type=F32,
    )
    slot = jnp.where(named, before, -1.0)
    scores = jnp.where(named, 1.0 / (1.0 + jnp.exp(-logits)), 0.0)
    weight = 2.5 * scores / jnp.sum(scores, axis=0, keepdims=True)
    meta = jnp.concatenate(
        [slot, weight, jnp.zeros((128 - 2 * experts, tok_count), F32)], axis=0
    ).astype(BF16)
    meta = lax.dot_general(
        (rows == cols).astype(F32).astype(BF16), meta, by_feature, preferred_element_type=F32
    )
    meta = meta.astype(BF16)
    swapped = place[0] == 1
    low, high = normed[:, :width], normed[:, width:]
    mine = jnp.where(swapped, high, low)
    out[:, :width] = mine
    out[:, width:model_width] = jnp.where(swapped, low, high)
    out[:, model_width:] = meta
    first[:, : width // 2] = mine[:, : width // 2]
    first[:, width // 2 :] = meta
    second[...] = mine[:, width // 2 :]


def prepare(experts, place, tokens, norm_gain, router, expert_ids):
    tok_count, model_width = tokens.shape
    arrays = (tokens, norm_gain, router.T, expert_ids.T)
    return pl.pallas_call(
        functools.partial(prepare_body, experts),
        out_shape=[
            jax.ShapeDtypeStruct((tok_count, columns), BF16)
            for columns in (model_width + 128, model_width // 4 + 128, model_width // 4)
        ],
        in_specs=[pl.BlockSpec(memory_space=pltpu.SMEM)] + [pl.BlockSpec(memory_space=pl.ANY)] * 4,
        out_specs=[pl.BlockSpec(memory_space=pltpu.VMEM)] * 3,
        scratch_shapes=[pltpu.VMEM(a.shape, a.dtype) for a in arrays]
        + [pltpu.SemaphoreType.DMA((4,))],
        compiler_params=pltpu.CompilerParams(vmem_limit_bytes=60 * 1024 * 1024),
        name="prepare",
    )(place, *arrays)


def mlp_body(plan, steps, carried, outs, columns, hand, place, *refs):
    count = 1 + max(piece for _, where in plan for piece, _ in where.values())
    pieces, (w_gate, w_up, w_down) = refs[:count], refs[count : count + 3]
    refs = refs[count + 3 :]
    before = refs[:2] if carried else ()
    refs = refs[2:] if carried else refs
    results, (gate_w, up_w, down_w, in_sems, down_sems) = refs[:-5], refs[-5:]
    model_width, hidden_width = w_gate.shape[1], w_gate.shape[2]
    step = gate_w.shape[1]
    total = model_width // step

    def start_of(first):
        moved = jnp.where(place[0] == first // (model_width // 2), 0, model_width // 2)
        return pl.multiple_of(moved + first % (model_width // 2), 128)

    def load(at, number):
        rows = pl.ds(start_of(number * step), step)
        return (
            pltpu.make_async_copy(w_gate.at[0, rows, :], gate_w.at[at], in_sems.at[0, at]),
            pltpu.make_async_copy(w_up.at[0, rows, :], up_w.at[at], in_sems.at[1, at]),
        )

    def load_down(number):
        first, size = columns[number]
        return pltpu.make_async_copy(
            w_down.at[0, :, pl.ds(start_of(first), size)],
            down_w.at[:, pl.ds(first, size)],
            down_sems.at[number],
        )

    for at, number in enumerate(steps):
        for copy in load(at, number):
            copy.start()
    for number in range(len(columns)):
        load_down(number).start()
    gates, ups = [], []
    first = 0
    for rows, _ in plan:
        for sums, ref in zip((gates, ups), before or (None, None)):
            zero = jnp.zeros((rows, hidden_width), F32)
            sums.append(zero if ref is None else ref[first : first + rows, :])
        first += rows
    for at, number in enumerate(steps):
        for copy in load(at, number):
            copy.wait()
        for b, (_, where) in enumerate(plan):
            piece, column = where[number]
            x = pieces[piece][:, column : column + step]
            gates[b] += jnp.dot(x, gate_w[at], preferred_element_type=F32)
            ups[b] += jnp.dot(x, up_w[at], preferred_element_type=F32)
    if not outs:
        first = 0
        for gate, up in zip(gates, ups):
            for ref, value in zip(results, (gate, up)):
                ref[first : first + value.shape[0], :] = value
            first += gate.shape[0]
        return
    hidden = [(g / (1.0 + jnp.exp(-g)) * u).astype(BF16) for g, u in zip(gates, ups)]
    if hand:
        results[-1][...] = hidden[0]
    for number, (left, size) in enumerate(columns):
        load_down(number).wait()
        first = 0
        for h in hidden:
            y = jnp.dot(h, down_w[:, left : left + size], preferred_element_type=F32).astype(BF16)
            for (start, rows, out_left, out_size), ref in zip(outs, results):
                low, high = max(start, first), min(start + rows, first + h.shape[0])
                if out_left <= left < out_left + out_size and low < high:
                    at = left - out_left
                    ref[low - start : high - start, at : at + size] = y[low - first : high - first]
            first += h.shape[0]


def mlp(place, blocks, steps, before, w_gate, w_up, w_down, outs, columns, hand=False):
    _, model_width, hidden_width = w_gate.shape
    total = 4
    step = model_width // total
    plan, pieces = [], []
    for block in blocks:
        where = {}
        for piece, covers in block:
            for at, number in enumerate(covers):
                where[number] = (len(pieces), at * step)
            pieces.append(piece)
        plan.append((block[0][0].shape[0], where))
    rows = sum(r for r, _ in plan)
    vmem = pl.BlockSpec(memory_space=pltpu.VMEM)
    if outs:
        shapes = [jax.ShapeDtypeStruct((r, c), BF16) for _, r, _, c in outs]
        shapes += [jax.ShapeDtypeStruct((rows, hidden_width), BF16)] * hand
    else:
        shapes = [jax.ShapeDtypeStruct((rows, hidden_width), F32)] * 2
    return pl.pallas_call(
        functools.partial(mlp_body, plan, steps, bool(before), outs, columns, hand),
        out_shape=shapes,
        in_specs=[pl.BlockSpec(memory_space=pltpu.SMEM)]
        + [vmem] * len(pieces)
        + [pl.BlockSpec(memory_space=pl.ANY)] * 3
        + [vmem] * len(before),
        out_specs=[vmem] * len(shapes),
        scratch_shapes=[
            pltpu.VMEM((len(steps), step, hidden_width), BF16),
            pltpu.VMEM((len(steps), step, hidden_width), BF16),
            pltpu.VMEM((hidden_width, model_width if outs else 128), BF16),
            pltpu.SemaphoreType.DMA((2, len(steps))),
            pltpu.SemaphoreType.DMA((max(1, len(columns)),)),
        ],
        compiler_params=pltpu.CompilerParams(vmem_limit_bytes=40 * 1024 * 1024),
        cost_estimate=pl.CostEstimate(
            flops=4 * rows * step * len(steps) * hidden_width
            + (2 * rows * model_width * hidden_width if outs else 0),
            bytes_accessed=4 * step * len(steps) * hidden_width
            + (2 * model_width * hidden_width if outs else 0),
            transcendentals=rows * hidden_width if outs else 0,
        ),
        name="mlp",
    )(place, *pieces, w_gate, w_up, w_down, *before)


def down_body(columns, place, hidden, w_down, *refs):
    outs, (weights, sems) = refs[: len(columns)], refs[len(columns) :]
    width = w_down.shape[2] // 2
    copies = []
    for number, (first, size) in enumerate(columns):
        moved = jnp.where(place[0] == first // width, 0, width) + first % width
        copies.append(pltpu.make_async_copy(
            w_down.at[0, :, pl.ds(pl.multiple_of(moved, 128), size)],
            weights.at[:, pl.ds(first, size)],
            sems.at[number],
        ))
    for copy in copies:
        copy.start()
    for copy, (first, size), out in zip(copies, columns, outs):
        copy.wait()
        out[...] = jnp.dot(
            hidden[...], weights[:, first : first + size], preferred_element_type=F32
        ).astype(BF16)


def down(place, hidden, w_down, columns):
    rows, hidden_width = hidden.shape
    vmem = pl.BlockSpec(memory_space=pltpu.VMEM)
    count = sum(size for _, size in columns)
    return pl.pallas_call(
        functools.partial(down_body, columns),
        out_shape=[jax.ShapeDtypeStruct((rows, size), BF16) for _, size in columns],
        in_specs=[pl.BlockSpec(memory_space=pltpu.SMEM), vmem, pl.BlockSpec(memory_space=pl.ANY)],
        out_specs=[vmem] * len(columns),
        scratch_shapes=[
            pltpu.VMEM((hidden_width, w_down.shape[2]), BF16),
            pltpu.SemaphoreType.DMA((len(columns),)),
        ],
        compiler_params=pltpu.CompilerParams(vmem_limit_bytes=40 * 1024 * 1024),
        cost_estimate=pl.CostEstimate(
            flops=2 * rows * count * hidden_width,
            bytes_accessed=2 * count * hidden_width,
            transcendentals=0,
        ),
        name="down",
    )(place, hidden, w_down)


def two_sections(experts, tokens, norm_gain, router, w_gate, w_up, w_down, expert_ids):
    tok_count, model_width = tokens.shape
    top_count = expert_ids.shape[1]
    cap = tok_count * top_count * 3 // (2 * experts)
    width = model_width // 2
    half = experts // 2
    chips = experts // 4
    me = lax.axis_index("expert")
    section = lax.axis_index("section")
    place = jnp.reshape(section, (1,)).astype(jnp.int32)
    group = 2 * cap

    def swap(value, mask):
        return lax.ppermute(value, "expert", [(i, i ^ mask) for i in range(experts)])

    def cross(value):
        return lax.ppermute(value, "section", [(0, 1), (1, 0)])

    packed, mine_0, mine_1 = prepare(experts, place, tokens, norm_gain, router, expert_ids)
    beside = swap(packed, 1)

    near = (((me // 2) ^ jnp.arange(chips, dtype=jnp.int32)) * 2 + me % 2)[:, None]
    lanes = jnp.arange(128, dtype=jnp.int32)[None, :]
    near = jnp.concatenate([near == lanes, near + experts == lanes], axis=0).astype(BF16)
    row = lax.broadcasted_iota(jnp.int32, (1, group, 2 * tok_count), 1)
    col = lax.broadcasted_iota(jnp.int32, (1, group, 2 * tok_count), 2)
    wanted = jnp.where(row // cap == col // tok_count, row % cap, -2).astype(F32)

    def tables(first, second):
        found = jnp.concatenate(
            [
                lax.dot_general(near, m, (((1,), (1,)), ((), ())), preferred_element_type=F32)
                for m in (first, second)
            ],
            axis=1,
        )
        chosen = found[:chips, None, :] == wanted
        factors = jnp.where(chosen, found[chips:, None, :], 0.0).astype(BF16)
        return chosen.astype(BF16), factors.reshape(chips * group, 2 * tok_count)

    def pick(chosen, first, second):
        flat = chosen.reshape(-1, 2 * tok_count)
        return (
            jnp.dot(flat[:, :tok_count], first, preferred_element_type=F32)
            + jnp.dot(flat[:, tok_count:], second, preferred_element_type=F32)
        ).astype(BF16)

    def pieces_of(rows, number):
        return [rows[q * group : (q + 1) * group] for q in range(number)]

    def spread(pieces):
        return [swap(piece, 2 * q) if q else piece for q, piece in enumerate(pieces)]

    def mix(factors, rows):
        return lax.dot_general(
            factors, rows, (((0,), (0,)), ((), ())), preferred_element_type=F32
        )

    def stage(*values):
        return lax.optimization_barrier(values)

    def core_sum(mixed):
        got = swap(mixed[tok_count:].astype(BF16), 1)
        return mixed[:tok_count], got

    weights = (w_gate, w_up, w_down)
    part = width // 2
    meta = packed[:, model_width:]
    far_0 = swap(mine_0, half)

    chosen, factors = tables(meta, beside[:, model_width:])
    some = pieces_of(pick(chosen[2:], packed[:, :width], beside[:, :width]), chips - 2)
    whole = pick(chosen[:2], packed[:, :model_width], beside[:, :model_width])
    far_1 = swap(stage(mine_1, some)[0], half)
    some = [swap(piece, 2 * q) for q, piece in enumerate(some, 2)]
    whole_near = swap(whole[group:], 2)
    whole_0 = whole[:group]
    some, far_0, far_1 = stage(some, far_0, far_1)

    some = jnp.concatenate(some, axis=0)
    some_other = cross(some)
    beside_0 = swap(far_0, 1)
    far_chosen, far_factors = tables(far_0[:, part:], beside_0[:, part:])
    rows_0 = spread(pieces_of(pick(far_chosen, far_0[:, :part], beside_0[:, :part]), chips))
    some, rows_0, whole_near = stage(some, rows_0, whole_near)

    rows_0 = jnp.concatenate(rows_0, axis=0)
    other_0 = cross(rows_0)
    rows_1 = spread(pieces_of(pick(far_chosen, far_1, swap(far_1, 1)), chips))
    whole = jnp.concatenate([whole_0, whole_near], axis=0)
    all_rows = chips * group
    (near,) = mlp(
        place, [[(whole, (0, 1, 2, 3))], [(some, (0, 1)), (some_other, (2, 3))]],
        (0, 1, 2, 3), (), *weights, [(0, all_rows, 0, model_width)],
        [(k * part, part) for k in range(4)],
    )
    rows_0, rows_1, near = stage(rows_0, rows_1, near)

    rows_1 = jnp.concatenate(rows_1, axis=0)
    other_1 = cross(rows_1)
    near = pieces_of(near, chips)
    near_back = near[:1] + [swap(near[q], 2 * q) for q in range(1, chips - 1)]
    near_last = swap(near[-1], 2 * (chips - 1))
    sums = mlp(
        place, [[(rows_0, (0,)), (rows_1, (1,)), (other_0, (2,))]], (0, 1, 2), (), *weights, (), ()
    )
    other_1, near_back, sums = stage(other_1, near_back, sums)

    lead = min(width - 128, (LEAD * width // 14 + 127) // 128 * 128)
    columns = [(width + lead, width - lead), (0, lead), (lead, width - lead)]
    give_0, hidden = mlp(
        place, [[(other_1, (3,))]], (3,), sums, *weights,
        [(0, all_rows, width, lead)], [(width, lead)], True,
    )
    give_0, hidden, near_back = stage(give_0, hidden, near_back)
    got_0 = cross(give_0)
    give_1, keep_0, keep_1 = down(place, hidden, w_down, columns)
    got_0, near_last, near_back, give_1 = stage(got_0, near_last, near_back, give_1)
    got_1 = cross(give_1)

    back_0 = spread(pieces_of((keep_0.astype(F32) + got_0.astype(F32)).astype(BF16), chips))
    near_sum = mix(factors, jnp.concatenate(near_back + [near_last], axis=0))
    far_0, far_0_core = core_sum(mix(far_factors, jnp.concatenate(back_0, axis=0)))
    got_1, far_0, far_0_core, near_sum = stage(got_1, far_0, far_0_core, near_sum)

    far_0 = swap((far_0 + far_0_core.astype(F32)).astype(BF16), half)
    back_1 = spread(pieces_of((keep_1.astype(F32) + got_1.astype(F32)).astype(BF16), chips))
    near_sum, near_core = core_sum(near_sum)
    far_1, far_1_core = core_sum(mix(far_factors, jnp.concatenate(back_1, axis=0)))
    near_sum, near_core, far_0, far_1, far_1_core = stage(near_sum, near_core, far_0, far_1, far_1_core)

    far_1 = (far_1 + far_1_core.astype(F32)).astype(BF16)
    far_1 = swap(far_1, half)
    near_sum = near_sum + near_core.astype(F32)
    near_got = cross(near_sum[:, width:].astype(BF16))
    residual = lax.dynamic_slice_in_dim(tokens, section * width, width, 1)
    near_sum = residual.astype(F32) + near_sum[:, :width] + near_got.astype(F32)
    first = (near_sum[:, :lead] + far_0.astype(F32)).astype(BF16)
    first, rest = stage(first, near_sum[:, lead:])
    return jnp.concatenate([first, (rest + far_1.astype(F32)).astype(BF16)], axis=1)


def solution(mesh):
    placed = (
        P("expert", None),
        P(),
        P(),
        P("expert", None, "section"),
        P("expert", None, "section"),
        P("expert", "section", None),
        P("expert", None),
    )

    def body(*args):
        sections, experts = mesh.shape["section"], mesh.shape["expert"]
        if sections == 2 and experts <= 64:
            return two_sections(experts, *args)
        return any_sections(sections, experts, *args)

    return jax.shard_map(
        body, mesh=mesh, in_specs=placed, out_specs=P("expert", "section"), check_vma=False
    )
```

```python
import functools

import jax
import jax.numpy as jnp
from jax import lax
from jax.experimental import pallas as pl
from jax.experimental.pallas import tpu as pltpu
from jax.sharding import PartitionSpec as P

EPSILON = 1e-06
LEAD = 8
F32, BF16 = jnp.float32, jnp.bfloat16


def any_sections(sections, experts, tokens, norm_gain, router, w_gate, w_up, w_down, expert_ids):
    tok_count, model_width = tokens.shape
    top_count = expert_ids.shape[1]
    cap = tok_count * top_count * 3 // (2 * experts)
    width = model_width // sections
    half = experts // 2
    chips = experts // 4
    me = lax.axis_index("expert")
    section = lax.axis_index("section")

    def swap(value, mask):
        return lax.ppermute(value, "expert", [(i, i ^ mask) for i in range(experts)])

    tokens_f = tokens.astype(F32)
    mean_sq = jnp.mean(tokens_f * tokens_f, axis=-1, keepdims=True)
    normed = (tokens_f * lax.rsqrt(mean_sq + EPSILON) * norm_gain.astype(F32)).astype(BF16)
    mine = lax.dynamic_slice_in_dim(normed, section * width, width, 1)

    def table(ids):
        named = jnp.any(ids[:, :, None] == jnp.arange(experts, dtype=jnp.int32), axis=1)
        rows = lax.broadcasted_iota(jnp.int32, (tok_count, tok_count), 0)
        cols = lax.broadcasted_iota(jnp.int32, (tok_count, tok_count), 1)
        before = jnp.dot(
            (cols < rows).astype(BF16), named.astype(BF16), preferred_element_type=F32
        )
        return named, jnp.where(named, before, -1.0)

    ids_core = swap(expert_ids, 1)
    ids_far = swap(expert_ids, half)
    ids_far_core = swap(expert_ids, half + 1)
    named, table_own = table(expert_ids)
    logits = jnp.dot(normed, router, preferred_element_type=F32)
    scores = jnp.where(named, jax.nn.sigmoid(logits), 0.0)
    weight = 2.5 * scores / jnp.sum(scores, axis=1, keepdims=True)
    weight_core = swap(weight, 1)
    weight_far = swap(weight, half)
    weight_far_core = swap(weight, half + 1)

    near = (((me // 2) ^ jnp.arange(chips, dtype=jnp.int32)) * 2 + me % 2)[:, None]
    near = (near == jnp.arange(experts, dtype=jnp.int32)[None, :]).astype(F32)

    def columns(first, second):
        both = jnp.concatenate([first, second], axis=0)
        return lax.dot_general(
            near, both, (((1,), (1,)), ((), ())), precision=lax.Precision.HIGHEST,
            preferred_element_type=F32,
        )

    row = lax.broadcasted_iota(jnp.int32, (1, 2 * cap, 2 * tok_count), 1)
    col = lax.broadcasted_iota(jnp.int32, (1, 2 * cap, 2 * tok_count), 2)
    wanted = jnp.where(row // cap == col // tok_count, row % cap, -2).astype(F32)

    def choose(first, second):
        return columns(first, second)[:, None, :] == wanted

    def pick(chosen, toks):
        flat = chosen.astype(BF16).reshape(chips * 2 * cap, 2 * tok_count)
        return jnp.dot(flat, toks, preferred_element_type=F32).astype(BF16).reshape(
            chips, 2 * cap, toks.shape[1]
        )

    def spread(rows):
        return jnp.concatenate(
            [rows[:1]] + [swap(rows[q : q + 1], 2 * q) for q in range(1, chips)], axis=0
        )

    def feature_exchange(rows):
        rows = rows.reshape(chips * 2 * cap, rows.shape[2])
        if sections == 2:
            other = lax.ppermute(rows, "section", [(0, 1), (1, 0)])
            low = jnp.where(section == 0, rows, other)
            high = jnp.where(section == 0, other, rows)
            return jnp.concatenate([low, high], axis=1)
        return lax.all_gather(rows, "section", axis=1, tiled=True)

    def experts_of(full):
        gate_act = jnp.dot(full, w_gate[0], preferred_element_type=F32)
        up_act = jnp.dot(full, w_up[0], preferred_element_type=F32)
        hidden = (jax.nn.silu(gate_act) * up_act).astype(BF16)
        part = jnp.dot(hidden, w_down[0], preferred_element_type=F32).astype(BF16)
        if sections == 2:
            keep = lax.dynamic_slice_in_dim(part, section * width, width, 1)
            give = lax.dynamic_slice_in_dim(part, (1 - section) * width, width, 1)
            got = lax.ppermute(give, "section", [(0, 1), (1, 0)])
            done = (keep.astype(F32) + got.astype(F32)).astype(BF16)
        else:
            done = lax.psum_scatter(part, "section", scatter_dimension=1, tiled=True)
        return done.reshape(chips, 2 * cap, width)

    def mix(chosen, first, second, rows):
        factors = jnp.where(chosen, columns(first, second)[:, None, :], 0.0).astype(BF16)
        factors = factors.reshape(chips * 2 * cap, 2 * tok_count)
        both = lax.dot_general(
            factors, rows.reshape(chips * 2 * cap, width), (((0,), (0,)), ((), ())),
            preferred_element_type=F32,
        )
        got = swap(both[tok_count:].astype(BF16), 1)
        return both[:tok_count] + got.astype(F32)

    chosen_near = choose(table_own, table(ids_core)[1])
    toks_near = jnp.concatenate([mine, swap(mine, 1)], axis=0)
    full_near = feature_exchange(spread(pick(chosen_near, toks_near)))
    far = swap(mine, half)
    chosen_far = choose(table(ids_far)[1], table(ids_far_core)[1])
    toks_far = jnp.concatenate([far, swap(far, 1)], axis=0)
    full_far = feature_exchange(spread(pick(chosen_far, toks_far)))

    back_near = spread(experts_of(full_near))
    back_far = spread(experts_of(full_far))
    sum_far = swap(mix(chosen_far, weight_far, weight_far_core, back_far).astype(BF16), half)
    sum_near = mix(chosen_near, weight, weight_core, back_near)
    residual = lax.dynamic_slice_in_dim(tokens, section * width, width, 1)
    return (residual.astype(F32) + sum_near + sum_far.astype(F32)).astype(BF16)


def prepare_body(experts, place, *refs):
    out, first, second = refs[4:7]
    tokens, gain, router, ids, sems = refs[7:]
    copies = [
        pltpu.make_async_copy(source, target, sems.at[i])
        for i, (source, target) in enumerate(zip(refs[:4], refs[7:11]))
    ]
    for copy in copies:
        copy.start()
    for copy in copies:
        copy.wait()
    tok_count, model_width = tokens.shape
    width = model_width // 2
    tokens_f = tokens[...].astype(F32)
    mean_sq = jnp.mean(tokens_f * tokens_f, axis=-1, keepdims=True)
    gain_f = gain[...].reshape(1, model_width).astype(F32)
    normed = (tokens_f * lax.rsqrt(mean_sq + EPSILON) * gain_f).astype(BF16)
    by_feature = (((1,), (1,)), ((), ()))
    logits = lax.dot_general(router[...], normed, by_feature, preferred_element_type=F32)
    expert = lax.broadcasted_iota(jnp.int32, (experts, tok_count), 0)
    named = ids[0:1, :] == expert
    for k in range(1, ids.shape[0]):
        named = named | (ids[k : k + 1, :] == expert)
    rows = lax.broadcasted_iota(jnp.int32, (tok_count, tok_count), 0)
    cols = lax.broadcasted_iota(jnp.int32, (tok_count, tok_count), 1)
    before = jnp.dot(
        named.astype(F32).astype(BF16),
        (rows < cols).astype(F32).astype(BF16),
        preferred_element_type=F32,
    )
    slot = jnp.where(named, before, -1.0)
    scores = jnp.where(named, 1.0 / (1.0 + jnp.exp(-logits)), 0.0)
    weight = 2.5 * scores / jnp.sum(scores, axis=0, keepdims=True)
    meta = jnp.concatenate(
        [slot, weight, jnp.zeros((128 - 2 * experts, tok_count), F32)], axis=0
    ).astype(BF16)
    meta = lax.dot_general(
        (rows == cols).astype(F32).astype(BF16), meta, by_feature, preferred_element_type=F32
    )
    meta = meta.astype(BF16)
    swapped = place[0] == 1
    low, high = normed[:, :width], normed[:, width:]
    mine = jnp.where(swapped, high, low)
    out[:, :width] = mine
    out[:, width:model_width] = jnp.where(swapped, low, high)
    out[:, model_width:] = meta
    first[:, : width // 2] = mine[:, : width // 2]
    first[:, width // 2 :] = meta
    second[...] = mine[:, width // 2 :]


def prepare(experts, place, tokens, norm_gain, router, expert_ids):
    tok_count, model_width = tokens.shape
    arrays = (tokens, norm_gain, router.T, expert_ids.T)
    return pl.pallas_call(
        functools.partial(prepare_body, experts),
        out_shape=[
            jax.ShapeDtypeStruct((tok_count, columns), BF16)
            for columns in (model_width + 128, model_width // 4 + 128, model_width // 4)
        ],
        in_specs=[pl.BlockSpec(memory_space=pltpu.SMEM)] + [pl.BlockSpec(memory_space=pl.ANY)] * 4,
        out_specs=[pl.BlockSpec(memory_space=pltpu.VMEM)] * 3,
        scratch_shapes=[pltpu.VMEM(a.shape, a.dtype) for a in arrays]
        + [pltpu.SemaphoreType.DMA((4,))],
        compiler_params=pltpu.CompilerParams(vmem_limit_bytes=60 * 1024 * 1024),
        name="prepare",
    )(place, *arrays)


def mlp_body(plan, steps, carried, outs, columns, hand, place, *refs):
    count = 1 + max(piece for _, where in plan for piece, _ in where.values())
    pieces, (w_gate, w_up, w_down) = refs[:count], refs[count : count + 3]
    refs = refs[count + 3 :]
    before = refs[:2] if carried else ()
    refs = refs[2:] if carried else refs
    results, (gate_w, up_w, down_w, in_sems, down_sems) = refs[:-5], refs[-5:]
    model_width, hidden_width = w_gate.shape[1], w_gate.shape[2]
    step = gate_w.shape[1]
    total = model_width // step

    def start_of(first):
        moved = jnp.where(place[0] == first // (model_width // 2), 0, model_width // 2)
        return pl.multiple_of(moved + first % (model_width // 2), 128)

    def load(at, number):
        rows = pl.ds(start_of(number * step), step)
        return (
            pltpu.make_async_copy(w_gate.at[0, rows, :], gate_w.at[at], in_sems.at[0, at]),
            pltpu.make_async_copy(w_up.at[0, rows, :], up_w.at[at], in_sems.at[1, at]),
        )

    def load_down(number):
        first, size = columns[number]
        return pltpu.make_async_copy(
            w_down.at[0, :, pl.ds(start_of(first), size)],
            down_w.at[:, pl.ds(first, size)],
            down_sems.at[number],
        )

    for at, number in enumerate(steps):
        for copy in load(at, number):
            copy.start()
    for number in range(len(columns)):
        load_down(number).start()
    gates, ups = [], []
    first = 0
    for rows, _ in plan:
        for sums, ref in zip((gates, ups), before or (None, None)):
            zero = jnp.zeros((rows, hidden_width), F32)
            sums.append(zero if ref is None else ref[first : first + rows, :])
        first += rows
    for at, number in enumerate(steps):
        for copy in load(at, number):
            copy.wait()
        for b, (_, where) in enumerate(plan):
            piece, column = where[number]
            x = pieces[piece][:, column : column + step]
            gates[b] += jnp.dot(x, gate_w[at], preferred_element_type=F32)
            ups[b] += jnp.dot(x, up_w[at], preferred_element_type=F32)
    if not outs:
        first = 0
        for gate, up in zip(gates, ups):
            for ref, value in zip(results, (gate, up)):
                ref[first : first + value.shape[0], :] = value
            first += gate.shape[0]
        return
    hidden = [(g / (1.0 + jnp.exp(-g)) * u).astype(BF16) for g, u in zip(gates, ups)]
    if hand:
        results[-1][...] = hidden[0]
    for number, (left, size) in enumerate(columns):
        load_down(number).wait()
        first = 0
        for h in hidden:
            y = jnp.dot(h, down_w[:, left : left + size], preferred_element_type=F32).astype(BF16)
            for (start, rows, out_left, out_size), ref in zip(outs, results):
                low, high = max(start, first), min(start + rows, first + h.shape[0])
                if out_left <= left < out_left + out_size and low < high:
                    at = left - out_left
                    ref[low - start : high - start, at : at + size] = y[low - first : high - first]
            first += h.shape[0]


def mlp(place, blocks, steps, before, w_gate, w_up, w_down, outs, columns, hand=False):
    _, model_width, hidden_width = w_gate.shape
    total = 4
    step = model_width // total
    plan, pieces = [], []
    for block in blocks:
        where = {}
        for piece, covers in block:
            for at, number in enumerate(covers):
                where[number] = (len(pieces), at * step)
            pieces.append(piece)
        plan.append((block[0][0].shape[0], where))
    rows = sum(r for r, _ in plan)
    vmem = pl.BlockSpec(memory_space=pltpu.VMEM)
    if outs:
        shapes = [jax.ShapeDtypeStruct((r, c), BF16) for _, r, _, c in outs]
        shapes += [jax.ShapeDtypeStruct((rows, hidden_width), BF16)] * hand
    else:
        shapes = [jax.ShapeDtypeStruct((rows, hidden_width), F32)] * 2
    return pl.pallas_call(
        functools.partial(mlp_body, plan, steps, bool(before), outs, columns, hand),
        out_shape=shapes,
        in_specs=[pl.BlockSpec(memory_space=pltpu.SMEM)]
        + [vmem] * len(pieces)
        + [pl.BlockSpec(memory_space=pl.ANY)] * 3
        + [vmem] * len(before),
        out_specs=[vmem] * len(shapes),
        scratch_shapes=[
            pltpu.VMEM((len(steps), step, hidden_width), BF16),
            pltpu.VMEM((len(steps), step, hidden_width), BF16),
            pltpu.VMEM((hidden_width, model_width if outs else 128), BF16),
            pltpu.SemaphoreType.DMA((2, len(steps))),
            pltpu.SemaphoreType.DMA((max(1, len(columns)),)),
        ],
        compiler_params=pltpu.CompilerParams(vmem_limit_bytes=40 * 1024 * 1024),
        cost_estimate=pl.CostEstimate(
            flops=4 * rows * step * len(steps) * hidden_width
            + (2 * rows * model_width * hidden_width if outs else 0),
            bytes_accessed=4 * step * len(steps) * hidden_width
            + (2 * model_width * hidden_width if outs else 0),
            transcendentals=rows * hidden_width if outs else 0,
        ),
        name="mlp",
    )(place, *pieces, w_gate, w_up, w_down, *before)


def down_body(columns, place, hidden, w_down, *refs):
    outs, (weights, sems) = refs[: len(columns)], refs[len(columns) :]
    width = w_down.shape[2] // 2
    copies = []
    for number, (first, size) in enumerate(columns):
        moved = jnp.where(place[0] == first // width, 0, width) + first % width
        copies.append(pltpu.make_async_copy(
            w_down.at[0, :, pl.ds(pl.multiple_of(moved, 128), size)],
            weights.at[:, pl.ds(first, size)],
            sems.at[number],
        ))
    for copy in copies:
        copy.start()
    for copy, (first, size), out in zip(copies, columns, outs):
        copy.wait()
        out[...] = jnp.dot(
            hidden[...], weights[:, first : first + size], preferred_element_type=F32
        ).astype(BF16)


def down(place, hidden, w_down, columns):
    rows, hidden_width = hidden.shape
    vmem = pl.BlockSpec(memory_space=pltpu.VMEM)
    count = sum(size for _, size in columns)
    return pl.pallas_call(
        functools.partial(down_body, columns),
        out_shape=[jax.ShapeDtypeStruct((rows, size), BF16) for _, size in columns],
        in_specs=[pl.BlockSpec(memory_space=pltpu.SMEM), vmem, pl.BlockSpec(memory_space=pl.ANY)],
        out_specs=[vmem] * len(columns),
        scratch_shapes=[
            pltpu.VMEM((hidden_width, w_down.shape[2]), BF16),
            pltpu.SemaphoreType.DMA((len(columns),)),
        ],
        compiler_params=pltpu.CompilerParams(vmem_limit_bytes=40 * 1024 * 1024),
        cost_estimate=pl.CostEstimate(
            flops=2 * rows * count * hidden_width,
            bytes_accessed=2 * count * hidden_width,
            transcendentals=0,
        ),
        name="down",
    )(place, hidden, w_down)


def two_sections(experts, tokens, norm_gain, router, w_gate, w_up, w_down, expert_ids):
    tok_count, model_width = tokens.shape
    top_count = expert_ids.shape[1]
    cap = tok_count * top_count * 3 // (2 * experts)
    width = model_width // 2
    half = experts // 2
    chips = experts // 4
    me = lax.axis_index("expert")
    section = lax.axis_index("section")
    place = jnp.reshape(section, (1,)).astype(jnp.int32)
    group = 2 * cap

    def swap(value, mask):
        return lax.ppermute(value, "expert", [(i, i ^ mask) for i in range(experts)])

    def cross(value):
        return lax.ppermute(value, "section", [(0, 1), (1, 0)])

    packed, mine_0, mine_1 = prepare(experts, place, tokens, norm_gain, router, expert_ids)
    beside = swap(packed, 1)

    near = (((me // 2) ^ jnp.arange(chips, dtype=jnp.int32)) * 2 + me % 2)[:, None]
    lanes = jnp.arange(128, dtype=jnp.int32)[None, :]
    near = jnp.concatenate([near == lanes, near + experts == lanes], axis=0).astype(BF16)
    row = lax.broadcasted_iota(jnp.int32, (1, group, 2 * tok_count), 1)
    col = lax.broadcasted_iota(jnp.int32, (1, group, 2 * tok_count), 2)
    wanted = jnp.where(row // cap == col // tok_count, row % cap, -2).astype(F32)

    def tables(first, second):
        found = jnp.concatenate(
            [
                lax.dot_general(near, m, (((1,), (1,)), ((), ())), preferred_element_type=F32)
                for m in (first, second)
            ],
            axis=1,
        )
        chosen = found[:chips, None, :] == wanted
        factors = jnp.where(chosen, found[chips:, None, :], 0.0).astype(BF16)
        return chosen.astype(BF16), factors.reshape(chips * group, 2 * tok_count)

    def pick(chosen, first, second):
        flat = chosen.reshape(-1, 2 * tok_count)
        return (
            jnp.dot(flat[:, :tok_count], first, preferred_element_type=F32)
            + jnp.dot(flat[:, tok_count:], second, preferred_element_type=F32)
        ).astype(BF16)

    def pieces_of(rows, number):
        return [rows[q * group : (q + 1) * group] for q in range(number)]

    def spread(pieces):
        return [swap(piece, 2 * q) if q else piece for q, piece in enumerate(pieces)]

    def mix(factors, rows):
        return lax.dot_general(
            factors, rows, (((0,), (0,)), ((), ())), preferred_element_type=F32
        )

    def stage(*values):
        return lax.optimization_barrier(values)

    def core_sum(mixed):
        got = swap(mixed[tok_count:].astype(BF16), 1)
        return mixed[:tok_count], got

    weights = (w_gate, w_up, w_down)
    part = width // 2
    meta = packed[:, model_width:]
    far_0 = swap(mine_0, half)

    chosen, factors = tables(meta, beside[:, model_width:])
    some = pieces_of(pick(chosen[2:], packed[:, :width], beside[:, :width]), chips - 2)
    whole = pick(chosen[:2], packed[:, :model_width], beside[:, :model_width])
    far_1 = swap(stage(mine_1, some)[0], half)
    some = [swap(piece, 2 * q) for q, piece in enumerate(some, 2)]
    whole_near = swap(whole[group:], 2)
    whole_0 = whole[:group]
    some, far_0, far_1 = stage(some, far_0, far_1)

    some = jnp.concatenate(some, axis=0)
    some_other = cross(some)
    beside_0 = swap(far_0, 1)
    far_chosen, far_factors = tables(far_0[:, part:], beside_0[:, part:])
    rows_0 = spread(pieces_of(pick(far_chosen, far_0[:, :part], beside_0[:, :part]), chips))
    some, rows_0 = stage(some, rows_0)

    rows_0 = jnp.concatenate(rows_0, axis=0)
    other_0 = cross(rows_0)
    rows_1 = spread(pieces_of(pick(far_chosen, far_1, swap(far_1, 1)), chips))
    whole = jnp.concatenate([whole_0, whole_near], axis=0)
    all_rows = chips * group
    (near,) = mlp(
        place, [[(whole, (0, 1, 2, 3))], [(some, (0, 1)), (some_other, (2, 3))]],
        (0, 1, 2, 3), (), *weights, [(0, all_rows, 0, model_width)],
        [(k * part, part) for k in range(4)],
    )
    rows_0, rows_1, near = stage(rows_0, rows_1, near)

    rows_1 = jnp.concatenate(rows_1, axis=0)
    other_1 = cross(rows_1)
    near = pieces_of(near, chips)
    near_back = near[:1] + [swap(near[q], 2 * q) for q in range(1, chips - 1)]
    near_last = swap(near[-1], 2 * (chips - 1))
    sums = mlp(
        place, [[(rows_0, (0,)), (rows_1, (1,)), (other_0, (2,))]], (0, 1, 2), (), *weights, (), ()
    )
    other_1, near_back, sums = stage(other_1, near_back, sums)

    lead = min(width - 128, (LEAD * width // 14 + 127) // 128 * 128)
    columns = [(width + lead, width - lead), (0, lead), (lead, width - lead)]
    give_0, hidden = mlp(
        place, [[(other_1, (3,))]], (3,), sums, *weights,
        [(0, all_rows, width, lead)], [(width, lead)], True,
    )
    give_0, hidden, near_back = stage(give_0, hidden, near_back)
    got_0 = cross(give_0)
    give_1, keep_0, keep_1 = down(place, hidden, w_down, columns)
    got_0, near_last, near_back, give_1 = stage(got_0, near_last, near_back, give_1)
    got_1 = cross(give_1)

    back_0 = spread(pieces_of((keep_0.astype(F32) + got_0.astype(F32)).astype(BF16), chips))
    near_sum = mix(factors, jnp.concatenate(near_back + [near_last], axis=0))
    far_0, far_0_core = core_sum(mix(far_factors, jnp.concatenate(back_0, axis=0)))
    got_1, far_0, far_0_core, near_sum = stage(got_1, far_0, far_0_core, near_sum)

    far_0 = swap((far_0 + far_0_core.astype(F32)).astype(BF16), half)
    back_1 = spread(pieces_of((keep_1.astype(F32) + got_1.astype(F32)).astype(BF16), chips))
    near_sum, near_core = core_sum(near_sum)
    far_1, far_1_core = core_sum(mix(far_factors, jnp.concatenate(back_1, axis=0)))
    near_sum, near_core, far_0, far_1, far_1_core = stage(near_sum, near_core, far_0, far_1, far_1_core)

    far_1 = (far_1 + far_1_core.astype(F32)).astype(BF16)
    far_1 = swap(far_1, half)
    near_sum = near_sum + near_core.astype(F32)
    near_got = cross(near_sum[:, width:].astype(BF16))
    residual = lax.dynamic_slice_in_dim(tokens, section * width, width, 1)
    near_sum = residual.astype(F32) + near_sum[:, :width] + near_got.astype(F32)
    first = (near_sum[:, :lead] + far_0.astype(F32)).astype(BF16)
    first, rest = stage(first, near_sum[:, lead:])
    return jnp.concatenate([first, (rest + far_1.astype(F32)).astype(BF16)], axis=1)


def solution(mesh):
    placed = (
        P("expert", None),
        P(),
        P(),
        P("expert", None, "section"),
        P("expert", None, "section"),
        P("expert", "section", None),
        P("expert", None),
    )

    def body(*args):
        sections, experts = mesh.shape["section"], mesh.shape["expert"]
        if sections == 2 and experts <= 64:
            return two_sections(experts, *args)
        return any_sections(sections, experts, *args)

    return jax.shard_map(
        body, mesh=mesh, in_specs=placed, out_specs=P("expert", "section"), check_vma=False
    )
```
